128 devices in a mesh: dp: 8 (over z, core), fsdp: 16 (over y, x).
Axes of the slice: x: 4, y: 4, z: 4, core: 2. Of those that a mesh axis runs over, the one named last changes fastest.
Arguments:
- partials: bfloat16 [8, 64, 1024, 1024], P('dp', None, 'fsdp'), may hold values from -5 to 5
- first_moment: float32 [64, 1024, 1024], P('dp', 'fsdp'), may hold values from -6 to 6
- second_moment: float32 [64, 1024, 1024], P('dp', 'fsdp'), may hold values from 0.05 to 5
- step_counts: int32 [64], replicated, may hold values from 1 to 199
- owners: int32 [64], replicated, may hold values from 0 to 15, as said below
- left_basis: bfloat16 [8, 16, 1024, 1024], P('dp', 'fsdp'), may hold values from -0.1875 to 0.1875
- right_basis: bfloat16 [8, 16, 1024, 1024], P('dp', 'fsdp'), may hold values from -0.1875 to 0.1875
Outputs:
- update: bfloat16 [64, 1024, 1024], P('dp', 'fsdp')
- new_first: float32 [64, 1024, 1024], P('dp', 'fsdp')
- new_second: float32 [64, 1024, 1024], P('dp', 'fsdp')
The draws below stay inside these ranges and needn't reach their ends.
Inputs may be any that keep to these rules, and one draw needn't show every extreme that they name: Within each aligned group of 8 blocks (blocks g * 8 to g * 8 + 7) the owners are distinct fsdp indices.
All inputs are finite; a program needn't handle non-finite values.
Results may differ from the reference program's by a relative error of at most 0.017.
Values may be sent and summed in bfloat16 or wider, within the bound.
A program may use at most 192 MiB of HBM per device.

```python
import math
import jax
import jax.numpy as jnp
from jax import lax

BS = 1024
NBD = 8
NB = 64
N_DP = 8
N_FSDP = 16


def draw_owners(key, part):
    key = jax.random.fold_in(key, 7)

    def one_group(group_index):
        return jax.random.permutation(jax.random.fold_in(key, group_index), N_FSDP)[:NBD]
    return jax.vmap(one_group)(jnp.arange(NB // NBD)).reshape(-1).astype(jnp.int32)


def with_ends(values, stream_key, least, top_value):
    index_at = [jax.random.randint(jax.random.fold_in(stream_key, axis), (), 0, length) for axis, length in enumerate(values.shape)]
    longest = values.shape.index(max(values.shape))
    beside = index_at[:longest] + [(index_at[longest] + 1) % values.shape[longest]] + index_at[longest + 1:]
    return values.at[tuple(index_at)].set(least).at[tuple(beside)].set(top_value)


def level_of(key, dims, cuts, low, largest):
    def one(axis_at, shards_of):
        steps = jax.random.uniform(jax.random.fold_in(jax.random.fold_in(key, 6), axis_at), (shards_of,), jnp.float32, low / len(cuts), largest / len(cuts))
        return jnp.repeat(jnp.exp(steps), dims[axis_at] // shards_of).reshape((-1,) + (1,) * (len(dims) - axis_at - 1))

    factor_of = one(*cuts[0])
    for cut in cuts[1:]:
        factor_of = factor_of * one(*cut)
    return factor_of


def normal_values(own_key, shape, width, most, pieces=(), kind=jnp.bfloat16):
    result = jax.random.normal(own_key, shape, jnp.float32) * width
    if len(pieces) > 0:
        result = level_of(own_key, shape, pieces, -0.22, 0.18) * result
    return jnp.clip(result, min=-most, max=most).astype(kind)


def setup_inputs(seed: int = 0) -> dict:
    arg_keys = jax.random.split(jax.random.key(seed), 8)
    return {
        "partials": normal_values(arg_keys[0], (N_DP, NB, BS, BS), 0.35, 5.0, ((0, 8), (2, 16))),
        "first_moment": normal_values(arg_keys[1], (NB, BS, BS), 0.5, 6.0, ((0, 8), (1, 16)), jnp.float32),
        "second_moment": jnp.clip(jnp.exp(math.log(5.0) - 4.6051702 * jax.random.uniform(arg_keys[2], (NB, BS, BS), jnp.float32) ** level_of(arg_keys[2], (NB, BS, BS), ((0, 8), (1, 16)), -0.2, 0.2)), 0.05, 5.0),
        "step_counts": with_ends(jax.random.randint(arg_keys[3], (NB,), 1, 200), jax.random.fold_in(arg_keys[3], 1), 1, 199).astype(jnp.int32),
        "owners": draw_owners(jax.random.fold_in(arg_keys[7], 71), 0),
        "left_basis": normal_values(arg_keys[5], (N_DP, N_FSDP, BS, BS), BS ** -0.5, 0.1875, ((0, 8), (1, 16))),
        "right_basis": normal_values(arg_keys[6], (N_DP, N_FSDP, BS, BS), BS ** -0.5, 0.1875, ((0, 8), (1, 16))),
    }


BETA_ONE = 0.9
BETA_TWO = 0.95
EPSILON = 1e-08

def adam_step(rotated, first_moment, second_moment, step_count):
    moment_one = BETA_ONE * first_moment + (1.0 - BETA_ONE) * rotated
    moment_two = BETA_TWO * second_moment + (1.0 - BETA_TWO) * rotated * rotated
    correct_one = 1.0 - jnp.power(BETA_ONE, step_count)
    correct_two = 1.0 - jnp.power(BETA_TWO, step_count)
    direction = (moment_one / correct_one / (jnp.sqrt(moment_two / correct_two) + EPSILON)).astype(jnp.bfloat16)
    return (direction, moment_one, moment_two)

def turn_forward(left_matrix, gradient, right_matrix):
    half_turn = lax.dot_general(left_matrix, gradient, (((0,), (0,)), ((), ())), preferred_element_type=jnp.float32).astype(jnp.bfloat16)
    return jnp.dot(half_turn, right_matrix, preferred_element_type=jnp.float32)

def turn_back(left_matrix, direction, right_matrix):
    half_turn = jnp.dot(left_matrix, direction, preferred_element_type=jnp.float32).astype(jnp.bfloat16)
    return lax.dot_general(half_turn, right_matrix, (((1,), (1,)), ((), ())), preferred_element_type=jnp.float32).astype(jnp.bfloat16)

def reference(partials, first_moment, second_moment, step_counts, owners, left_basis, right_basis):

    def one_block(block_index):
        group_index = block_index // NBD
        member_index = owners[block_index]
        left_matrix = left_basis[group_index, member_index]
        right_matrix = right_basis[group_index, member_index]
        gradient = lax.optimization_barrier(jnp.sum(partials[:, block_index].astype(jnp.float32), axis=0)).astype(jnp.bfloat16)
        rotated = turn_forward(left_matrix, gradient, right_matrix)
        step_count = step_counts[block_index].astype(jnp.float32)
        direction, moment_one, moment_two = adam_step(rotated, first_moment[block_index], second_moment[block_index], step_count)
        return (turn_back(left_matrix, direction, right_matrix), moment_one, moment_two)
    update, new_first, new_second = lax.map(one_block, jnp.arange(NB, dtype=jnp.int32))
    return (update, new_first, new_second)
```

```python
import functools
import math

import jax
import jax.numpy as jnp
from jax import lax
from jax.experimental import pallas as pl
from jax.experimental.pallas import tpu as pltpu
from jax.sharding import PartitionSpec as P

BETA_ONE = 0.9
BETA_TWO = 0.95
EPSILON = 1e-08
MESH = pl.DeviceIdType.MESH
F32 = jnp.float32
BF16 = jnp.bfloat16

NZ = 4
SIDE = 4
NF = SIDE * SIDE
NBD = 8
ROWS = 64
BS = 1024
GROUP = SIDE * ROWS
NCH = 4
CW = BS // NCH
KEEP = 32
BACK = ROWS - KEEP


def new_moments(first, second, rotated):
    moment_one = BETA_ONE * first + (1.0 - BETA_ONE) * rotated
    moment_two = BETA_TWO * second + (1.0 - BETA_TWO) * (rotated * rotated)
    return moment_one, moment_two


def direction_of(moment_one, moment_two, scale_one, scale_two):
    return ((moment_one * scale_one) / (jnp.sqrt(moment_two * scale_two) + EPSILON)).astype(BF16)


def wait_bytes(ref, sem):
    pltpu.make_async_copy(ref, ref, sem).wait()


def kernel(
    owners, counts, part, first, second, left, right,
    out_u, out_m, out_v,
    slot_s, owner_s, scale_one, scale_two,
    own, other, relay_s, relay_r, toward_s, toward_r, summed, grad_s, grad_r,
    lmat, lturn, rmat, half, mom_m, mom_v, ahead_s, ahead_r,
    rot_s, rot_r, dir_s, dir_r, upd_s, upd_r, new_m, new_v, new_u,
    ld_sem, in_sem, core_ss, core_rs, relay_ss, relay_rs, toward_ss, toward_rs,
    grad_ss, grad_rs, ahead_ss, ahead_rs, rot_ss, rot_rs, dir_ss, dir_rs, upd_ss, upd_rs, out_sem,
):
    dp = lax.axis_index("dp")
    me = lax.axis_index("fsdp")
    z, core = dp // 2, dp % 2
    y, x = me // SIDE, me % SIDE
    up, down, far = (z + 1) % NZ, (z + NZ - 1) % NZ, (z + 2) % NZ
    dev_core = (z * 2 + 1 - core, me)
    dev_up = (up * 2 + core, me)
    dev_down = (down * 2 + core, me)

    def peer(index):
        return (dp, index)

    def loop(count, body):
        def step(i, carry):
            body(i)
            return carry

        lax.fori_loop(0, count, step, 0)

    def cols(k):
        return pl.ds(pl.multiple_of(k * CW, CW), CW)

    def load_own(k):
        return pltpu.make_async_copy(part.at[:, core, :, :, cols(k)], own.at[k], ld_sem.at[k])

    in_copies = [
        pltpu.make_async_copy(first, mom_m, in_sem.at[0]),
        pltpu.make_async_copy(second, mom_v, in_sem.at[1]),
        pltpu.make_async_copy(left, lmat, in_sem.at[2]),
        pltpu.make_async_copy(right, rmat, in_sem.at[3]),
    ]
    load_own(0).start()
    load_own(1).start()

    barrier = pltpu.get_barrier_semaphore()
    for device in (dev_core, dev_up, dev_down):
        pl.semaphore_signal(barrier, inc=1, device_id=device, device_id_type=MESH)

    def greet(d):
        pl.semaphore_signal(
            barrier, inc=1, device_id=peer((me + d + 1) % NF), device_id_type=MESH
        )

    loop(NF - 1, greet)

    def find_slots(j):
        slot = jnp.int32(0)
        for b in range(NBD):
            slot = jnp.where(owners[dp * NBD + b] == j, jnp.int32(b), slot)
        slot_s[j] = slot

    loop(NF, find_slots)

    def find_scales(b):
        owner_s[b] = owners[dp * NBD + b]
        count = jnp.full((1, BS), counts[dp * NBD + b].astype(F32), F32)
        scale_one[b] = 1.0 / (1.0 - jnp.exp(count * math.log(BETA_ONE)))
        scale_two[b] = 1.0 / (1.0 - jnp.exp(count * math.log(BETA_TWO)))

    loop(NBD, find_scales)
    pl.semaphore_wait(barrier, NF + 2)

    def send_core(k):
        for zz in (far, up, down, z):
            pltpu.make_async_remote_copy(
                src_ref=part.at[zz, 1 - core, :, :, cols(k)],
                dst_ref=other.at[k, zz],
                send_sem=core_ss,
                recv_sem=core_rs.at[k, zz],
                device_id=dev_core,
                device_id_type=MESH,
            ).start()

    def pair(k, zz, b):
        return own[k, zz, b].astype(F32) + other[k, zz, b].astype(F32)

    def send_toward(k, side, at, device):
        pltpu.make_async_remote_copy(
            src_ref=toward_s.at[k, side, pl.ds(at, NBD // 2)],
            dst_ref=toward_r.at[k, side, pl.ds(at, NBD // 2)],
            send_sem=toward_ss,
            recv_sem=toward_rs.at[k],
            device_id=device,
            device_id_type=MESH,
        ).start()

    hb = NBD // 2

    def sum_far(k):
        load_own(k).wait()
        wait_bytes(other.at[k, far], core_rs.at[k, far])
        for side, device in ((0, dev_up), (1, dev_down)):

            def body(b):
                relay_s[k, side, b] = pair(k, far, side * hb + b).astype(BF16)

            loop(hb, body)
            pltpu.make_async_remote_copy(
                src_ref=relay_s.at[k, side],
                dst_ref=relay_r.at[k, side],
                send_sem=relay_ss,
                recv_sem=relay_rs.at[k, side],
                device_id=device,
                device_id_type=MESH,
            ).start()

    def sum_near(k):
        for side, zz, device in ((0, up, dev_up), (1, down, dev_down)):
            wait_bytes(other.at[k, zz], core_rs.at[k, zz])
            at = (1 - side) * hb

            def body(b):
                toward_s[k, side, at + b] = pair(k, zz, at + b).astype(BF16)

            loop(hb, body)
            send_toward(k, side, at, device)

    def sum_relayed(k):
        for side, zz, device in ((0, up, dev_up), (1, down, dev_down)):
            wait_bytes(relay_r.at[k, side], relay_rs.at[k, side])
            at = side * hb

            def body(b):
                toward_s[k, side, at + b] = (
                    pair(k, zz, at + b) + relay_r[k, side, b].astype(F32)
                ).astype(BF16)

            loop(hb, body)
            send_toward(k, side, at, device)

    def send_grad(k):
        wait_bytes(other.at[k, z], core_rs.at[k, z])
        wait_bytes(toward_r.at[k], toward_rs.at[k])

        def body(b):
            summed[b] = (
                pair(k, z, b) + toward_r[k, 0, b].astype(F32) + toward_r[k, 1, b].astype(F32)
            ).astype(BF16)

        loop(NBD, body)

        def send(d):
            j = (me + d + 1) % NF
            grad_s[k, j] = summed[slot_s[j]]
            pltpu.make_async_remote_copy(
                src_ref=grad_s.at[k, j],
                dst_ref=grad_r.at[k, me],
                send_sem=grad_ss,
                recv_sem=grad_rs.at[k],
                device_id=peer(j),
                device_id_type=MESH,
            ).start()

        loop(NF - 1, send)
        grad_r[k, me] = summed[slot_s[me]]

    def turn_left(k):
        wait_bytes(grad_r.at[k, pl.ds(0, NF - 1)], grad_rs.at[k])

        def body(q):
            rows = pl.ds(pl.multiple_of(q * GROUP, GROUP), GROUP)
            half[rows, cols(k)] = jnp.dot(
                lturn[rows, :], grad_r[k].reshape(BS, CW), preferred_element_type=F32
            ).astype(BF16)

        loop(SIDE, body)

    def send_ahead():
        in_copies[0].wait()
        in_copies[1].wait()

        def send(d):
            j = (me + d) % NF
            slot = slot_s[j]
            ahead_s[j, 0] = mom_m[slot][:KEEP].astype(BF16)
            ahead_s[j, 1] = mom_v[slot][:KEEP].astype(BF16)

            @pl.when(j != me)
            def _():
                pltpu.make_async_remote_copy(
                    src_ref=ahead_s.at[j],
                    dst_ref=ahead_r.at[me],
                    send_sem=ahead_ss,
                    recv_sem=ahead_rs,
                    device_id=peer(j),
                    device_id_type=MESH,
                ).start()

            @pl.when(j == me)
            def _():
                ahead_r[me] = ahead_s[me]

        loop(NF, send)

    def turn_basis():
        in_copies[2].wait()
        in_copies[3].wait()

        def body(q):
            rows = pl.ds(pl.multiple_of(q * GROUP, GROUP), GROUP)
            lturn[rows, :] = lmat[:, rows].T

        loop(SIDE, body)

    def chunk(t):
        @pl.when(t + 2 < NCH)
        def _():
            load_own(t + 2).start()
            send_core(t + 2)

        @pl.when(t < NCH)
        def _():
            sum_far(t)
            sum_near(t)

        @pl.when(t == 0)
        def _():
            send_ahead()
            turn_basis()

        @pl.when((t >= 1) & (t < NCH + 1))
        def _():
            sum_relayed(t - 1)

        @pl.when((t >= 2) & (t < NCH + 2))
        def _():
            send_grad(t - 2)

        @pl.when(t >= 3)
        def _():
            turn_left(t - 3)

    send_core(0)
    send_core(1)
    for copy in in_copies:
        copy.start()
    loop(NCH + 3, chunk)

    my_slot = slot_s[me]
    wait_bytes(ahead_r.at[pl.ds(0, NF - 1)], ahead_rs)

    def turn_right(q):
        yy = (y + 1 + q) % SIDE
        rows = pl.ds(pl.multiple_of(yy * GROUP, GROUP), GROUP)
        rot_s[pl.ds(yy * SIDE, SIDE)] = (
            jnp.dot(half[rows, :], rmat[...], preferred_element_type=F32)
            .astype(BF16)
            .reshape(SIDE, ROWS, BS)
        )

        def send(xx):
            j = yy * SIDE + xx

            @pl.when(j != me)
            def _():
                pltpu.make_async_remote_copy(
                    src_ref=rot_s.at[j],
                    dst_ref=rot_r.at[me],
                    send_sem=rot_ss,
                    recv_sem=rot_rs.at[me],
                    device_id=peer(j),
                    device_id_type=MESH,
                ).start()

            @pl.when(j == me)
            def _():
                rot_r[me] = rot_s[me]

        loop(SIDE, send)

    loop(SIDE, turn_right)

    def direct_ahead(i):
        one, two = scale_one[my_slot], scale_two[my_slot]
        for at in range(0, KEEP, 16):
            rows = pl.ds(at, 16)
            moment_one, moment_two = new_moments(
                ahead_r[i, 0, rows].astype(F32),
                ahead_r[i, 1, rows].astype(F32),
                rot_s[i, rows].astype(F32),
            )
            dir_r[i, rows] = direction_of(moment_one, moment_two, one, two)

    loop(NF, direct_ahead)

    def direct(q):
        jy = (y + 2 * SIDE - 1 - q) % SIDE

        def answer(xx):
            j = jy * SIDE + xx
            slot = slot_s[j]

            @pl.when(j != me)
            def _():
                wait_bytes(rot_r.at[j], rot_rs.at[j])

            one, two = scale_one[slot], scale_two[slot]
            for at in range(0, BACK, 16):
                rows = pl.ds(KEEP + at, 16)
                moment_one, moment_two = new_moments(
                    mom_m[slot, rows], mom_v[slot, rows], rot_r[j, rows].astype(F32)
                )
                dir_s[j, pl.ds(at, 16)] = direction_of(moment_one, moment_two, one, two)

            @pl.when(j != me)
            def _():
                pltpu.make_async_remote_copy(
                    src_ref=dir_s.at[j],
                    dst_ref=dir_r.at[me, pl.ds(KEEP, BACK)],
                    send_sem=dir_ss,
                    recv_sem=dir_rs.at[me],
                    device_id=peer(j),
                    device_id_type=MESH,
                ).start()

            @pl.when(j == me)
            def _():
                dir_r[me, pl.ds(KEEP, BACK)] = dir_s[me]

        loop(SIDE, answer)

    def back_right(q):
        yy = (y + 1 + q) % SIDE

        def arrive(xx):
            i = yy * SIDE + xx

            @pl.when(i != me)
            def _():
                wait_bytes(dir_r.at[i, pl.ds(KEEP, BACK)], dir_rs.at[i])

        loop(SIDE, arrive)
        rows = pl.ds(pl.multiple_of(yy * GROUP, GROUP), GROUP)
        half[rows, :] = lax.dot_general(
            dir_r[pl.ds(yy * SIDE, SIDE)].reshape(GROUP, BS),
            rmat[...],
            (((1,), (1,)), ((), ())),
            preferred_element_type=F32,
        ).astype(BF16)

    def back(q):
        @pl.when(q < SIDE)
        def _():
            direct(q)

        @pl.when(q >= 1)
        def _():
            back_right(q - 1)

    loop(SIDE + 1, back)

    def back_left(q):
        yy = (y + 1 + q) % SIDE
        rows = pl.ds(pl.multiple_of(yy * GROUP, GROUP), GROUP)
        upd_s[pl.ds(yy * SIDE, SIDE)] = (
            jnp.dot(lmat[rows, :], half[...], preferred_element_type=F32)
            .astype(BF16)
            .reshape(SIDE, ROWS, BS)
        )

        def send(xx):
            j = yy * SIDE + xx

            @pl.when(j != me)
            def _():
                pltpu.make_async_remote_copy(
                    src_ref=upd_s.at[j],
                    dst_ref=upd_r.at[me],
                    send_sem=upd_ss,
                    recv_sem=upd_rs,
                    device_id=peer(j),
                    device_id_type=MESH,
                ).start()

            @pl.when(j == me)
            def _():
                upd_r[me] = upd_s[me]

        loop(SIDE, send)

    loop(SIDE, back_left)

    def keep(b):
        owner = owner_s[b]
        for at in range(0, ROWS, 16):
            rows = pl.ds(at, 16)
            new_m[b, rows], new_v[b, rows] = new_moments(
                mom_m[b, rows], mom_v[b, rows], rot_r[owner, rows].astype(F32)
            )

    loop(NBD, keep)
    save_m = pltpu.make_async_copy(new_m, out_m, out_sem.at[0])
    save_v = pltpu.make_async_copy(new_v, out_v, out_sem.at[1])
    save_m.start()
    save_v.start()

    wait_bytes(upd_r.at[pl.ds(0, NF - 1)], upd_rs)

    def take(b):
        new_u[b] = upd_r[owner_s[b]]

    loop(NBD, take)
    save_u = pltpu.make_async_copy(new_u, out_u, out_sem.at[2])
    save_u.start()

    wait_bytes(other, core_ss)
    wait_bytes(relay_s, relay_ss)
    wait_bytes(toward_s, toward_ss)
    wait_bytes(grad_s.at[:, pl.ds(0, NF - 1)], grad_ss)
    wait_bytes(ahead_s.at[pl.ds(0, NF - 1)], ahead_ss)
    wait_bytes(rot_s.at[pl.ds(0, NF - 1)], rot_ss)
    wait_bytes(dir_s.at[pl.ds(0, NF - 1)], dir_ss)
    wait_bytes(upd_s.at[pl.ds(0, NF - 1)], upd_ss)
    save_m.wait()
    save_v.wait()
    save_u.wait()


def shards(partials, first_moment, second_moment, step_counts, owners, left_basis, right_basis):
    part = partials.reshape(NZ, 2, NBD, ROWS, BS)
    strips = (NBD, ROWS, BS)
    slots = (NF, ROWS, BS)
    any_space = pl.BlockSpec(memory_space=pl.ANY)
    scalars = pl.BlockSpec(memory_space=pltpu.SMEM)
    dma = pltpu.SemaphoreType.DMA
    return pl.pallas_call(
        kernel,
        out_shape=(
            jax.ShapeDtypeStruct(strips, BF16),
            jax.ShapeDtypeStruct(strips, F32),
            jax.ShapeDtypeStruct(strips, F32),
        ),
        in_specs=[scalars] * 2 + [any_space] * 5,
        out_specs=(any_space,) * 3,
        scratch_shapes=[
            pltpu.SMEM((NF,), jnp.int32),
            pltpu.SMEM((NBD,), jnp.int32),
            pltpu.VMEM((NBD, 1, BS), F32),
            pltpu.VMEM((NBD, 1, BS), F32),
            pltpu.VMEM((NCH, NZ, NBD, ROWS, CW), BF16),
            pltpu.VMEM((NCH, NZ, NBD, ROWS, CW), BF16),
            pltpu.VMEM((NCH, 2, NBD // 2, ROWS, CW), BF16),
            pltpu.VMEM((NCH, 2, NBD // 2, ROWS, CW), BF16),
            pltpu.VMEM((NCH, 2, NBD, ROWS, CW), BF16),
            pltpu.VMEM((NCH, 2, NBD, ROWS, CW), BF16),
            pltpu.VMEM((NBD, ROWS, CW), BF16),
            pltpu.VMEM((NCH, NF, ROWS, CW), BF16),
            pltpu.VMEM((NCH, NF, ROWS, CW), BF16),
            pltpu.VMEM((BS, BS), BF16),
            pltpu.VMEM((BS, BS), BF16),
            pltpu.VMEM((BS, BS), BF16),
            pltpu.VMEM((BS, BS), BF16),
            pltpu.VMEM(strips, F32),
            pltpu.VMEM(strips, F32),
            pltpu.VMEM((NF, 2, KEEP, BS), BF16),
            pltpu.VMEM((NF, 2, KEEP, BS), BF16),
            pltpu.VMEM(slots, BF16),
            pltpu.VMEM(slots, BF16),
            pltpu.VMEM((NF, BACK, BS), BF16),
            pltpu.VMEM(slots, BF16),
            pltpu.VMEM(slots, BF16),
            pltpu.VMEM(slots, BF16),
            pltpu.VMEM(strips, F32),
            pltpu.VMEM(strips, F32),
            pltpu.VMEM(strips, BF16),
            dma((NCH,)),
            dma((4,)),
            dma,
            dma((NCH, NZ)),
            dma,
            dma((NCH, 2)),
            dma,
            dma((NCH,)),
            dma,
            dma((NCH,)),
            dma,
            dma,
            dma,
            dma((NF,)),
            dma,
            dma((NF,)),
            dma,
            dma,
            dma((3,)),
        ],
        compiler_params=pltpu.CompilerParams(
            collective_id=0, has_side_effects=True, vmem_limit_bytes=60 * 2**20
        ),
        name="soap_step",
    )(owners, step_counts, part, first_moment, second_moment, left_basis[0, 0], right_basis[0, 0])


def solution(mesh):
    placed = (
        P("dp", None, "fsdp", None),
        P("dp", "fsdp", None),
        P("dp", "fsdp", None),
        P(),
        P(),
        P("dp", "fsdp", None, None),
        P("dp", "fsdp", None, None),
    )
    return jax.shard_map(
        shards,
        mesh=mesh,
        in_specs=placed,
        out_specs=(P("dp", "fsdp", None), P("dp", "fsdp", None), P("dp", "fsdp", None)),
        check_vma=False,
    )
```

```python
import functools
import math

import jax
import jax.numpy as jnp
from jax import lax
from jax.experimental import pallas as pl
from jax.experimental.pallas import tpu as pltpu
from jax.sharding import PartitionSpec as P

BETA_ONE = 0.9
BETA_TWO = 0.95
EPSILON = 1e-08
MESH = pl.DeviceIdType.MESH
F32 = jnp.float32
BF16 = jnp.bfloat16

NZ = 4
SIDE = 4
NF = SIDE * SIDE
NBD = 8
ROWS = 64
BS = 1024
GROUP = SIDE * ROWS
NCH = 8
CW = BS // NCH
PAIR = 2
KEEP = 16
BACK = ROWS - KEEP
PIECE = ROWS // 2
TURNS = (2, 1, 3, 0)
PARTS = (
    ((2, 2), (2, 1), (2, 3)),
    ((1, 2), (1, 1), (1, 3)),
    ((3, 2), (3, 3), (3, 1), (2, 0)),
    ((0, 2), (1, 0), (3, 0), (0, 1), (0, 3)),
)
ORDER = sum(PARTS, ())


def new_moments(first, second, rotated):
    moment_one = BETA_ONE * first + (1.0 - BETA_ONE) * rotated
    moment_two = BETA_TWO * second + (1.0 - BETA_TWO) * (rotated * rotated)
    return moment_one, moment_two


def direction_of(moment_one, moment_two, scale_one, scale_two):
    return ((moment_one * scale_one) / (jnp.sqrt(moment_two * scale_two) + EPSILON)).astype(BF16)


def wait_bytes(ref, sem):
    pltpu.make_async_copy(ref, ref, sem).wait()


def kernel(
    owners, counts, part, first, second, left, right,
    rot_o, upd_r,
    slot_s, owner_s, scale_one, scale_two,
    own, other, relay_s, relay_r, toward_s, toward_r, summed, grad_s, grad_r,
    lmat, lturn, rmat, half, mom_m, mom_v, ahead_s, ahead_r,
    rot_s, rot_r, dir_s, dir_r, upd_s, strips,
    ld_sem, in_sem, core_ss, core_rs, relay_ss, relay_rs, toward_ss, toward_rs,
    grad_ss, grad_rs, ahead_ss, ahead_rs, rot_ss, rot_rs, kept_ss, kept_rs, dir_ss, dir_rs, upd_ss, upd_rs, out_sem,
):
    dp = lax.axis_index("dp")
    me = lax.axis_index("fsdp")
    z, core = dp // 2, dp % 2
    y, x = me // SIDE, me % SIDE
    up, down, far = (z + 1) % NZ, (z + NZ - 1) % NZ, (z + 2) % NZ
    dev_core = (z * 2 + 1 - core, me)
    dev_up = (up * 2 + core, me)
    dev_down = (down * 2 + core, me)

    def peer(index):
        return (dp, index)

    def loop(count, body):
        def step(i, carry):
            body(i)
            return carry

        lax.fori_loop(0, count, step, 0)

    def chosen(n, values):
        value = jnp.int32(values[0])
        for i, other_value in enumerate(values[1:]):
            value = jnp.where(n == i + 1, jnp.int32(other_value), value)
        return value

    def to_nth(n):
        yy = (y + chosen(n, [dy for dy, _ in ORDER])) % SIDE
        return yy * SIDE + (x + chosen(n, [dx for _, dx in ORDER])) % SIDE

    def from_nth(n):
        yy = (y + SIDE - chosen(n, [dy for dy, _ in ORDER])) % SIDE
        return yy * SIDE + (x + SIDE - chosen(n, [dx for _, dx in ORDER])) % SIDE

    def send_part(n, send):
        for i, part_n in enumerate(PARTS):

            @pl.when(n == i)
            def _():
                for dy, dx in part_n:
                    send(((y + dy) % SIDE) * SIDE + (x + dx) % SIDE)

    def turn_rows(n):
        yy = (y + chosen(n, TURNS)) % SIDE
        return yy, pl.ds(pl.multiple_of(yy * GROUP, GROUP), GROUP)

    def cols(k):
        return pl.ds(pl.multiple_of(k * CW, CW), CW)

    def load_own(k):
        return pltpu.make_async_copy(part.at[:, core, :, :, cols(k)], own.at[k], ld_sem.at[k])

    in_copies = [
        pltpu.make_async_copy(first, mom_m, in_sem.at[0]),
        pltpu.make_async_copy(second, mom_v, in_sem.at[1]),
        pltpu.make_async_copy(left, lmat, in_sem.at[2]),
        pltpu.make_async_copy(right, rmat, in_sem.at[3]),
    ]
    load_own(0).start()
    load_own(1).start()

    barrier = pltpu.get_barrier_semaphore()
    for device in (dev_core, dev_up, dev_down):
        pl.semaphore_signal(barrier, inc=1, device_id=device, device_id_type=MESH)

    def greet(d):
        pl.semaphore_signal(
            barrier, inc=1, device_id=peer((me + d + 1) % NF), device_id_type=MESH
        )

    loop(NF - 1, greet)

    def find_slots(j):
        slot = jnp.int32(0)
        for b in range(NBD):
            slot = jnp.where(owners[dp * NBD + b] == j, jnp.int32(b), slot)
        slot_s[j] = slot

    loop(NF, find_slots)

    def find_scales(b):
        owner_s[b] = owners[dp * NBD + b]
        count = jnp.full((1, BS), counts[dp * NBD + b].astype(F32), F32)
        scale_one[b] = 1.0 / (1.0 - jnp.exp(count * math.log(BETA_ONE)))
        scale_two[b] = 1.0 / (1.0 - jnp.exp(count * math.log(BETA_TWO)))

    loop(NBD, find_scales)
    pl.semaphore_wait(barrier, NF + 2)

    def send_core(k):
        for zz in (far, up, down, z):
            pltpu.make_async_remote_copy(
                src_ref=part.at[zz, 1 - core, :, :, cols(k)],
                dst_ref=other.at[k, zz],
                send_sem=core_ss,
                recv_sem=core_rs.at[k, zz],
                device_id=dev_core,
                device_id_type=MESH,
            ).start()

    def pair(k, zz, b):
        return own[k, zz, b].astype(F32) + other[k, zz, b].astype(F32)

    def send_toward(k, side, at, device):
        pltpu.make_async_remote_copy(
            src_ref=toward_s.at[k, side, pl.ds(at, NBD // 2)],
            dst_ref=toward_r.at[k, side, pl.ds(at, NBD // 2)],
            send_sem=toward_ss,
            recv_sem=toward_rs.at[k],
            device_id=device,
            device_id_type=MESH,
        ).start()

    hb = NBD // 2

    def sum_far(k):
        load_own(k).wait()
        wait_bytes(other.at[k, far], core_rs.at[k, far])
        for side, device in ((0, dev_up), (1, dev_down)):

            def body(b):
                relay_s[k, side, b] = pair(k, far, side * hb + b).astype(BF16)

            loop(hb, body)
            pltpu.make_async_remote_copy(
                src_ref=relay_s.at[k, side],
                dst_ref=relay_r.at[k, side],
                send_sem=relay_ss,
                recv_sem=relay_rs.at[k, side],
                device_id=device,
                device_id_type=MESH,
            ).start()

    def sum_near(k):
        for side, zz, device in ((0, up, dev_up), (1, down, dev_down)):
            wait_bytes(other.at[k, zz], core_rs.at[k, zz])
            at = (1 - side) * hb

            def body(b):
                toward_s[k, side, at + b] = pair(k, zz, at + b).astype(BF16)

            loop(hb, body)
            send_toward(k, side, at, device)

    def sum_relayed(k):
        for side, zz, device in ((0, up, dev_up), (1, down, dev_down)):
            wait_bytes(relay_r.at[k, side], relay_rs.at[k, side])
            at = side * hb

            def body(b):
                toward_s[k, side, at + b] = (
                    pair(k, zz, at + b) + relay_r[k, side, b].astype(F32)
                ).astype(BF16)

            loop(hb, body)
            send_toward(k, side, at, device)

    def send_grad(k):
        wait_bytes(other.at[k, z], core_rs.at[k, z])
        wait_bytes(toward_r.at[k], toward_rs.at[k])

        def body(b):
            summed[b] = (
                pair(k, z, b) + toward_r[k, 0, b].astype(F32) + toward_r[k, 1, b].astype(F32)
            ).astype(BF16)

        loop(NBD, body)

        def send(n):
            j = to_nth(n)
            grad_s[k, j] = summed[slot_s[j]]
            pltpu.make_async_remote_copy(
                src_ref=grad_s.at[k, j],
                dst_ref=grad_r.at[k, me],
                send_sem=grad_ss,
                recv_sem=grad_rs.at[k],
                device_id=peer(j),
                device_id_type=MESH,
            ).start()

        loop(NF - 1, send)
        grad_r[k, me] = summed[slot_s[me]]

    def turn_left(p):
        k = PAIR * p
        for n in range(PAIR):
            wait_bytes(grad_r.at[k + n, pl.ds(0, NF - 1)], grad_rs.at[k + n])

        def body(q):
            rows = pl.ds(pl.multiple_of(q * GROUP, GROUP), GROUP)
            grad = jnp.concatenate([grad_r[k + n].reshape(BS, CW) for n in range(PAIR)], axis=1)
            half[rows, pl.ds(pl.multiple_of(k * CW, PAIR * CW), PAIR * CW)] = jnp.dot(
                lturn[rows, :], grad, preferred_element_type=F32
            ).astype(BF16)

        loop(SIDE, body)

    def send_ahead():
        in_copies[0].wait()
        in_copies[1].wait()

        def pack(j):
            slot = slot_s[j]
            ahead_s[j, 0] = mom_m[slot][:KEEP].astype(BF16)
            ahead_s[j, 1] = mom_v[slot][:KEEP].astype(BF16)

        def send(n):
            j = to_nth(n)
            pack(j)
            pltpu.make_async_remote_copy(
                src_ref=ahead_s.at[j],
                dst_ref=ahead_r.at[me],
                send_sem=ahead_ss,
                recv_sem=ahead_rs,
                device_id=peer(j),
                device_id_type=MESH,
            ).start()

        loop(NF - 1, send)
        pack(me)
        ahead_r[me] = ahead_s[me]

    def turn_basis():
        in_copies[2].wait()
        in_copies[3].wait()

        def body(q):
            rows = pl.ds(pl.multiple_of(q * GROUP, GROUP), GROUP)
            lturn[rows, :] = lmat[:, rows].T

        loop(SIDE, body)

    def chunk(t):
        @pl.when(t + 2 < NCH)
        def _():
            load_own(t + 2).start()
            send_core(t + 2)

        @pl.when(t < NCH)
        def _():
            sum_far(t)
            sum_near(t)

        @pl.when(t == 0)
        def _():
            send_ahead()
            turn_basis()

        @pl.when((t >= 1) & (t < NCH + 1))
        def _():
            sum_relayed(t - 1)

        @pl.when(t >= 2)
        def _():
            send_grad(t - 2)

    send_core(0)
    send_core(1)
    for copy in in_copies:
        copy.start()
    loop(NCH + 2, chunk)
    loop(NCH // PAIR, turn_left)

    my_slot = slot_s[me]
    wait_bytes(ahead_r.at[pl.ds(0, NF - 1)], ahead_rs)

    def send_rotated(j):
        pltpu.make_async_remote_copy(
            src_ref=rot_s.at[j, pl.ds(KEEP, BACK)],
            dst_ref=rot_r.at[me, pl.ds(KEEP, BACK)],
            send_sem=rot_ss,
            recv_sem=rot_rs.at[me],
            device_id=peer(j),
            device_id_type=MESH,
        ).start()

    def send_kept(n):
        j = to_nth(n)
        pltpu.make_async_remote_copy(
            src_ref=rot_s.at[j, pl.ds(0, KEEP)],
            dst_ref=rot_r.at[me, pl.ds(0, KEEP)],
            send_sem=kept_ss,
            recv_sem=kept_rs,
            device_id=peer(j),
            device_id_type=MESH,
        ).start()

    def turn_right(n):
        yy, rows = turn_rows(n)
        rot_s[pl.ds(yy * SIDE, SIDE)] = (
            jnp.dot(half[rows, :], rmat[...], preferred_element_type=F32)
            .astype(BF16)
            .reshape(SIDE, ROWS, BS)
        )
        send_part(n, send_rotated)

    loop(SIDE, turn_right)
    rot_r[me] = rot_s[me]

    def direct_ahead(i):
        one, two = scale_one[my_slot], scale_two[my_slot]
        for at in range(0, KEEP, 16):
            rows = pl.ds(at, 16)
            moment_one, moment_two = new_moments(
                ahead_r[i, 0, rows].astype(F32),
                ahead_r[i, 1, rows].astype(F32),
                rot_s[i, rows].astype(F32),
            )
            dir_r[i, rows] = direction_of(moment_one, moment_two, one, two)

    loop(NF, direct_ahead)

    def direct(j):
        slot = slot_s[j]
        one, two = scale_one[slot], scale_two[slot]
        for at in range(0, BACK, 16):
            rows = pl.ds(KEEP + at, 16)
            moment_one, moment_two = new_moments(
                mom_m[slot, rows], mom_v[slot, rows], rot_r[j, rows].astype(F32)
            )
            dir_s[j, pl.ds(at, 16)] = direction_of(moment_one, moment_two, one, two)

    def answer(n):
        j = from_nth(n)
        wait_bytes(rot_r.at[j, pl.ds(KEEP, BACK)], rot_rs.at[j])
        direct(j)
        pltpu.make_async_remote_copy(
            src_ref=dir_s.at[j],
            dst_ref=dir_r.at[me, pl.ds(KEEP, BACK)],
            send_sem=dir_ss,
            recv_sem=dir_rs.at[me],
            device_id=peer(j),
            device_id_type=MESH,
        ).start()

    loop(NF - 1, answer)
    loop(NF - 1, send_kept)
    direct(me)
    dir_r[me, pl.ds(KEEP, BACK)] = dir_s[me]

    def back_right(n):
        yy, rows = turn_rows(n)

        def arrive(xx):
            i = yy * SIDE + xx

            @pl.when(i != me)
            def _():
                wait_bytes(dir_r.at[i, pl.ds(KEEP, BACK)], dir_rs.at[i])

        loop(SIDE, arrive)
        half[rows, :] = lax.dot_general(
            dir_r[pl.ds(yy * SIDE, SIDE)].reshape(GROUP, BS),
            rmat[...],
            (((1,), (1,)), ((), ())),
            preferred_element_type=F32,
        ).astype(BF16)

    loop(SIDE, back_right)

    def send_update(j, at):
        pltpu.make_async_remote_copy(
            src_ref=upd_s.at[j, pl.ds(at, PIECE)],
            dst_ref=upd_r.at[me, pl.ds(at, PIECE)],
            send_sem=upd_ss,
            recv_sem=upd_rs,
            device_id=peer(j),
            device_id_type=MESH,
        ).start()

    def back_left(n):
        yy, rows = turn_rows(n)
        upd_s[pl.ds(yy * SIDE, SIDE)] = (
            jnp.dot(lmat[rows, :], half[...], preferred_element_type=F32)
            .astype(BF16)
            .reshape(SIDE, ROWS, BS)
        )
        send_part(n, lambda j: send_update(j, 0))

    loop(SIDE, back_left)
    loop(NF - 1, lambda n: send_update(to_nth(n), PIECE))
    save_own = pltpu.make_async_copy(upd_s.at[me], upd_r.at[me], out_sem.at[1])
    save_own.start()

    wait_bytes(rot_r.at[pl.ds(0, NF - 1), pl.ds(0, KEEP)], kept_rs)

    def take(b):
        strips[b] = rot_r[owner_s[b]]

    loop(NBD, take)
    save = pltpu.make_async_copy(strips, rot_o, out_sem.at[0])
    save.start()
    wait_bytes(upd_s.at[pl.ds(0, NF - 1)], upd_rs)

    wait_bytes(other, core_ss)
    wait_bytes(relay_s, relay_ss)
    wait_bytes(toward_s, toward_ss)
    wait_bytes(grad_s.at[:, pl.ds(0, NF - 1)], grad_ss)
    wait_bytes(ahead_s.at[pl.ds(0, NF - 1)], ahead_ss)
    wait_bytes(rot_s.at[pl.ds(0, NF - 1), pl.ds(KEEP, BACK)], rot_ss)
    wait_bytes(rot_s.at[pl.ds(0, NF - 1), pl.ds(0, KEEP)], kept_ss)
    wait_bytes(dir_s.at[pl.ds(0, NF - 1)], dir_ss)
    wait_bytes(upd_s.at[pl.ds(0, NF - 1)], upd_ss)
    save.wait()
    save_own.wait()


def keep_kernel(
    owners, rot, upd, first, second, out_u, out_m, out_v,
    mom_m, mom_v, rows_r, rows_u, new_m, new_v, in_sem, out_sem,
):
    base = lax.axis_index("dp") * NBD
    copies = []
    for b in range(NBD):
        copies.append(
            [
                pltpu.make_async_copy(first.at[b], mom_m.at[b], in_sem.at[b, 0]),
                pltpu.make_async_copy(second.at[b], mom_v.at[b], in_sem.at[b, 1]),
                pltpu.make_async_copy(rot.at[b], rows_r.at[b], in_sem.at[b, 2]),
                pltpu.make_async_copy(upd.at[owners[base + b]], rows_u.at[b], in_sem.at[b, 3]),
            ]
        )
        for copy in copies[b]:
            copy.start()
    saves = []
    for b in range(NBD):
        for copy in copies[b]:
            copy.wait()

        def step(i, carry, b=b):
            rows = pl.ds(pl.multiple_of(i * 16, 16), 16)
            new_m[b, rows], new_v[b, rows] = new_moments(
                mom_m[b, rows], mom_v[b, rows], rows_r[b, rows].astype(F32)
            )
            return carry

        lax.fori_loop(0, ROWS // 16, step, 0)
        for n, (source, target) in enumerate(((rows_u, out_u), (new_m, out_m), (new_v, out_v))):
            saves.append(pltpu.make_async_copy(source.at[b], target.at[b], out_sem.at[b, n]))
            saves[-1].start()
    for save in saves:
        save.wait()


def shards(partials, first_moment, second_moment, step_counts, owners, left_basis, right_basis):
    part = partials.reshape(NZ, 2, NBD, ROWS, BS)
    strips = (NBD, ROWS, BS)
    slots = (NF, ROWS, BS)
    any_space = pl.BlockSpec(memory_space=pl.ANY)
    scalars = pl.BlockSpec(memory_space=pltpu.SMEM)
    dma = pltpu.SemaphoreType.DMA
    rotated, update = pl.pallas_call(
        kernel,
        out_shape=(jax.ShapeDtypeStruct(strips, BF16), jax.ShapeDtypeStruct(slots, BF16)),
        in_specs=[scalars] * 2 + [any_space] * 5,
        out_specs=(any_space,) * 2,
        scratch_shapes=[
            pltpu.SMEM((NF,), jnp.int32),
            pltpu.SMEM((NBD,), jnp.int32),
            pltpu.VMEM((NBD, 1, BS), F32),
            pltpu.VMEM((NBD, 1, BS), F32),
            pltpu.VMEM((NCH, NZ, NBD, ROWS, CW), BF16),
            pltpu.VMEM((NCH, NZ, NBD, ROWS, CW), BF16),
            pltpu.VMEM((NCH, 2, NBD // 2, ROWS, CW), BF16),
            pltpu.VMEM((NCH, 2, NBD // 2, ROWS, CW), BF16),
            pltpu.VMEM((NCH, 2, NBD, ROWS, CW), BF16),
            pltpu.VMEM((NCH, 2, NBD, ROWS, CW), BF16),
            pltpu.VMEM((NBD, ROWS, CW), BF16),
            pltpu.VMEM((NCH, NF, ROWS, CW), BF16),
            pltpu.VMEM((NCH, NF, ROWS, CW), BF16),
            pltpu.VMEM((BS, BS), BF16),
            pltpu.VMEM((BS, BS), BF16),
            pltpu.VMEM((BS, BS), BF16),
            pltpu.VMEM((BS, BS), BF16),
            pltpu.VMEM(strips, F32),
            pltpu.VMEM(strips, F32),
            pltpu.VMEM((NF, 2, KEEP, BS), BF16),
            pltpu.VMEM((NF, 2, KEEP, BS), BF16),
            pltpu.VMEM(slots, BF16),
            pltpu.VMEM(slots, BF16),
            pltpu.VMEM((NF, BACK, BS), BF16),
            pltpu.VMEM(slots, BF16),
            pltpu.VMEM(slots, BF16),
            pltpu.VMEM(strips, BF16),
            dma((NCH,)),
            dma((4,)),
            dma,
            dma((NCH, NZ)),
            dma,
            dma((NCH, 2)),
            dma,
            dma((NCH,)),
            dma,
            dma((NCH,)),
            dma,
            dma,
            dma,
            dma((NF,)),
            dma,
            dma,
            dma,
            dma((NF,)),
            dma,
            dma,
            dma((2,)),
        ],
        compiler_params=pltpu.CompilerParams(
            collective_id=0, has_side_effects=True, vmem_limit_bytes=60 * 2**20
        ),
        name="soap_step",
    )(owners, step_counts, part, first_moment, second_moment, left_basis[0, 0], right_basis[0, 0])
    return pl.pallas_call(
        keep_kernel,
        out_shape=(
            jax.ShapeDtypeStruct(strips, BF16),
            jax.ShapeDtypeStruct(strips, F32),
            jax.ShapeDtypeStruct(strips, F32),
        ),
        in_specs=[scalars] + [any_space] * 4,
        out_specs=(any_space,) * 3,
        scratch_shapes=[
            pltpu.VMEM(strips, F32),
            pltpu.VMEM(strips, F32),
            pltpu.VMEM(strips, BF16),
            pltpu.VMEM(strips, BF16),
            pltpu.VMEM(strips, F32),
            pltpu.VMEM(strips, F32),
            dma((NBD, 4)),
            dma((NBD, 3)),
        ],
        compiler_params=pltpu.CompilerParams(vmem_limit_bytes=60 * 2**20),
        name="keep_moments",
    )(owners, rotated, update, first_moment, second_moment)


def solution(mesh):
    placed = (
        P("dp", None, "fsdp", None),
        P("dp", "fsdp", None),
        P("dp", "fsdp", None),
        P(),
        P(),
        P("dp", "fsdp", None, None),
        P("dp", "fsdp", None, None),
    )
    return jax.shard_map(
        shards,
        mesh=mesh,
        in_specs=placed,
        out_specs=(P("dp", "fsdp", None), P("dp", "fsdp", None), P("dp", "fsdp", None)),
        check_vma=False,
    )
```

```python
import functools
import math

import jax
import jax.numpy as jnp
from jax import lax
from jax.experimental import pallas as pl
from jax.experimental.pallas import tpu as pltpu
from jax.sharding import PartitionSpec as P

BETA_ONE = 0.9
BETA_TWO = 0.95
EPSILON = 1e-08
MESH = pl.DeviceIdType.MESH
F32 = jnp.float32
BF16 = jnp.bfloat16

NZ = 4
SIDE = 4
NF = SIDE * SIDE
NBD = 8
ROWS = 64
BS = 1024
GROUP = SIDE * ROWS
NCH = 8
CW = BS // NCH
PAIR = 2
FIRST = BS - PAIR * CW
KEEP = 16
BACK = ROWS - KEEP
SLICE = 16
PIECE = ROWS // 2
TURNS = (2, 1, 3, 0)
PARTS = (
    ((2, 2), (2, 1), (2, 3)),
    ((1, 2), (1, 1), (1, 3)),
    ((3, 2), (3, 3), (3, 1), (2, 0)),
    ((0, 2), (1, 0), (3, 0), (0, 1), (0, 3)),
)
ORDER = sum(PARTS, ())


def new_moments(first, second, rotated):
    moment_one = BETA_ONE * first + (1.0 - BETA_ONE) * rotated
    moment_two = BETA_TWO * second + (1.0 - BETA_TWO) * (rotated * rotated)
    return moment_one, moment_two


def direction_of(moment_one, moment_two, scale_one, scale_two):
    return ((moment_one * scale_one) / (jnp.sqrt(moment_two * scale_two) + EPSILON)).astype(BF16)


def wait_bytes(ref, sem):
    pltpu.make_async_copy(ref, ref, sem).wait()


def kernel(
    owners, counts, part, first, second, left, right,
    out_u, out_m, out_v,
    slot_s, owner_s, scale_one, scale_two,
    own, other, relay_s, relay_r, toward_s, toward_r, summed, grad_s, grad_r,
    lmat, lturn, rmat, half, begun, mom_m, mom_v, ahead_s, ahead_r,
    rot_s, rot_r, dir_s, dir_r, upd_s, upd_r,
    ld_sem, in_sem, core_ss, core_rs, relay_ss, relay_rs, toward_ss, toward_rs,
    grad_ss, grad_rs, ahead_ss, ahead_rs, rot_ss, rot_rs, kept_ss, kept_rs, dir_ss, dir_rs, upd_ss, upd_rs,
):
    dp = lax.axis_index("dp")
    me = lax.axis_index("fsdp")
    z, core = dp // 2, dp % 2
    y, x = me // SIDE, me % SIDE
    up, down, far = (z + 1) % NZ, (z + NZ - 1) % NZ, (z + 2) % NZ
    dev_core = (z * 2 + 1 - core, me)
    dev_up = (up * 2 + core, me)
    dev_down = (down * 2 + core, me)

    def peer(index):
        return (dp, index)

    def loop(count, body):
        def step(i, carry):
            body(i)
            return carry

        lax.fori_loop(0, count, step, 0)

    def chosen(n, values):
        value = jnp.int32(values[0])
        for i, other_value in enumerate(values[1:]):
            value = jnp.where(n == i + 1, jnp.int32(other_value), value)
        return value

    def to_nth(n):
        yy = (y + chosen(n, [dy for dy, _ in ORDER])) % SIDE
        return yy * SIDE + (x + chosen(n, [dx for _, dx in ORDER])) % SIDE

    def from_nth(n):
        yy = (y + SIDE - chosen(n, [dy for dy, _ in ORDER])) % SIDE
        return yy * SIDE + (x + SIDE - chosen(n, [dx for _, dx in ORDER])) % SIDE

    def send_part(n, send):
        for i, part_n in enumerate(PARTS):

            @pl.when(n == i)
            def _():
                for dy, dx in part_n:
                    send(((y + dy) % SIDE) * SIDE + (x + dx) % SIDE)

    def turn_rows(n):
        yy = (y + chosen(n, TURNS)) % SIDE
        return yy, pl.ds(pl.multiple_of(yy * GROUP, GROUP), GROUP)

    def cols(k):
        return pl.ds(pl.multiple_of(k * CW, CW), CW)

    def load_own(k):
        return pltpu.make_async_copy(part.at[:, core, :, :, cols(k)], own.at[k], ld_sem.at[k])

    in_copies = [
        pltpu.make_async_copy(first, mom_m, in_sem.at[0]),
        pltpu.make_async_copy(second, mom_v, in_sem.at[1]),
        pltpu.make_async_copy(left, lmat, in_sem.at[2]),
        pltpu.make_async_copy(right, rmat, in_sem.at[3]),
    ]
    load_own(0).start()
    load_own(1).start()

    barrier = pltpu.get_barrier_semaphore()
    for device in (dev_core, dev_up, dev_down):
        pl.semaphore_signal(barrier, inc=1, device_id=device, device_id_type=MESH)

    def greet(d):
        pl.semaphore_signal(
            barrier, inc=1, device_id=peer((me + d + 1) % NF), device_id_type=MESH
        )

    loop(NF - 1, greet)

    def find_slots(j):
        slot = jnp.int32(0)
        for b in range(NBD):
            slot = jnp.where(owners[dp * NBD + b] == j, jnp.int32(b), slot)
        slot_s[j] = slot

    loop(NF, find_slots)

    def find_scales(b):
        owner_s[b] = owners[dp * NBD + b]
        count = jnp.full((1, BS), counts[dp * NBD + b].astype(F32), F32)
        scale_one[b] = 1.0 / (1.0 - jnp.exp(count * math.log(BETA_ONE)))
        scale_two[b] = 1.0 / (1.0 - jnp.exp(count * math.log(BETA_TWO)))

    loop(NBD, find_scales)
    pl.semaphore_wait(barrier, NF + 2)

    def send_core(k):
        for zz in (far, up, down, z):
            pltpu.make_async_remote_copy(
                src_ref=part.at[zz, 1 - core, :, :, cols(k)],
                dst_ref=other.at[k, zz],
                send_sem=core_ss,
                recv_sem=core_rs.at[k, zz],
                device_id=dev_core,
                device_id_type=MESH,
            ).start()

    def pair(k, zz, b):
        return own[k, zz, b].astype(F32) + other[k, zz, b].astype(F32)

    def send_toward(k, side, at, device):
        pltpu.make_async_remote_copy(
            src_ref=toward_s.at[k, side, pl.ds(at, NBD // 2)],
            dst_ref=toward_r.at[k, side, pl.ds(at, NBD // 2)],
            send_sem=toward_ss,
            recv_sem=toward_rs.at[k],
            device_id=device,
            device_id_type=MESH,
        ).start()

    hb = NBD // 2

    def sum_far(k):
        load_own(k).wait()
        wait_bytes(other.at[k, far], core_rs.at[k, far])
        for side, device in ((0, dev_up), (1, dev_down)):

            def body(b):
                relay_s[k, side, b] = pair(k, far, side * hb + b).astype(BF16)

            loop(hb, body)
            pltpu.make_async_remote_copy(
                src_ref=relay_s.at[k, side],
                dst_ref=relay_r.at[k, side],
                send_sem=relay_ss,
                recv_sem=relay_rs.at[k, side],
                device_id=device,
                device_id_type=MESH,
            ).start()

    def sum_near(k):
        for side, zz, device in ((0, up, dev_up), (1, down, dev_down)):
            wait_bytes(other.at[k, zz], core_rs.at[k, zz])
            at = (1 - side) * hb

            def body(b):
                toward_s[k, side, at + b] = pair(k, zz, at + b).astype(BF16)

            loop(hb, body)
            send_toward(k, side, at, device)

    def sum_relayed(k):
        for side, zz, device in ((0, up, dev_up), (1, down, dev_down)):
            wait_bytes(relay_r.at[k, side], relay_rs.at[k, side])
            at = side * hb

            def body(b):
                toward_s[k, side, at + b] = (
                    pair(k, zz, at + b) + relay_r[k, side, b].astype(F32)
                ).astype(BF16)

            loop(hb, body)
            send_toward(k, side, at, device)

    def send_grad(k):
        wait_bytes(other.at[k, z], core_rs.at[k, z])
        wait_bytes(toward_r.at[k], toward_rs.at[k])

        def body(b):
            summed[b] = (
                pair(k, z, b) + toward_r[k, 0, b].astype(F32) + toward_r[k, 1, b].astype(F32)
            ).astype(BF16)

        loop(NBD, body)

        def send(n):
            j = to_nth(n)
            grad_s[k, j] = summed[slot_s[j]]
            pltpu.make_async_remote_copy(
                src_ref=grad_s.at[k, j],
                dst_ref=grad_r.at[k, me],
                send_sem=grad_ss,
                recv_sem=grad_rs.at[k],
                device_id=peer(j),
                device_id_type=MESH,
            ).start()

        loop(NF - 1, send)
        grad_r[k, me] = summed[slot_s[me]]

    def turn_left(p):
        k = PAIR * p
        for n in range(PAIR):
            wait_bytes(grad_r.at[k + n, pl.ds(0, NF - 1)], grad_rs.at[k + n])

        def body(q):
            rows = pl.ds(pl.multiple_of(q * GROUP, GROUP), GROUP)
            grad = jnp.concatenate([grad_r[k + n].reshape(BS, CW) for n in range(PAIR)], axis=1)
            half[rows, pl.ds(pl.multiple_of(k * CW, PAIR * CW), PAIR * CW)] = jnp.dot(
                lturn[rows, :], grad, preferred_element_type=F32
            ).astype(BF16)

        loop(SIDE, body)

    def send_ahead():
        in_copies[0].wait()
        in_copies[1].wait()

        def pack(j):
            slot = slot_s[j]
            ahead_s[j, 0] = mom_m[slot][:KEEP].astype(BF16)
            ahead_s[j, 1] = mom_v[slot][:KEEP].astype(BF16)

        def send(n):
            j = to_nth(n)
            pack(j)
            pltpu.make_async_remote_copy(
                src_ref=ahead_s.at[j],
                dst_ref=ahead_r.at[me],
                send_sem=ahead_ss,
                recv_sem=ahead_rs,
                device_id=peer(j),
                device_id_type=MESH,
            ).start()

        loop(NF - 1, send)
        pack(me)
        ahead_r[me] = ahead_s[me]

    def turn_basis():
        in_copies[2].wait()
        in_copies[3].wait()

        def body(q):
            rows = pl.ds(pl.multiple_of(q * GROUP, GROUP), GROUP)
            lturn[rows, :] = lmat[:, rows].T

        loop(SIDE, body)

    def chunk(t):
        @pl.when(t + 2 < NCH)
        def _():
            load_own(t + 2).start()
            send_core(t + 2)

        @pl.when(t < NCH)
        def _():
            sum_far(t)
            sum_near(t)

        @pl.when(t == 0)
        def _():
            send_ahead()
            turn_basis()

        @pl.when((t >= 1) & (t < NCH + 1))
        def _():
            sum_relayed(t - 1)

        @pl.when(t >= 2)
        def _():
            send_grad(t - 2)

    send_core(0)
    send_core(1)
    for copy in in_copies:
        copy.start()
    loop(NCH + 2, chunk)
    loop(NCH // PAIR - 1, turn_left)

    def begin(q):
        rows = pl.ds(pl.multiple_of(q * GROUP, GROUP), GROUP)
        begun[rows, :] = jnp.dot(half[rows, :FIRST], rmat[:FIRST, :], preferred_element_type=F32)

    loop(SIDE, begin)
    turn_left(NCH // PAIR - 1)

    my_slot = slot_s[me]
    wait_bytes(ahead_r.at[pl.ds(0, NF - 1)], ahead_rs)

    def send_rotated(j, r):
        rows = pl.ds(KEEP + r * SLICE, SLICE)
        pltpu.make_async_remote_copy(
            src_ref=rot_s.at[j, rows],
            dst_ref=rot_r.at[me, rows],
            send_sem=rot_ss,
            recv_sem=rot_rs.at[r, me],
            device_id=peer(j),
            device_id_type=MESH,
        ).start()

    def send_kept(n):
        j = to_nth(n)
        pltpu.make_async_remote_copy(
            src_ref=rot_s.at[j, pl.ds(0, KEEP)],
            dst_ref=rot_r.at[me, pl.ds(0, KEEP)],
            send_sem=kept_ss,
            recv_sem=kept_rs,
            device_id=peer(j),
            device_id_type=MESH,
        ).start()

    def turn_right(n):
        yy, rows = turn_rows(n)
        rot_s[pl.ds(yy * SIDE, SIDE)] = (
            (begun[rows, :] + jnp.dot(half[rows, FIRST:], rmat[FIRST:, :], preferred_element_type=F32))
            .astype(BF16)
            .reshape(SIDE, ROWS, BS)
        )
        send_part(n, lambda j: send_rotated(j, 0))

    loop(SIDE, turn_right)
    for r in range(1, BACK // SLICE):
        loop(NF - 1, lambda n, r=r: send_rotated(to_nth(n), r))
    rot_r[me] = rot_s[me]

    def direct_ahead(i):
        one, two = scale_one[my_slot], scale_two[my_slot]
        for at in range(0, KEEP, 16):
            rows = pl.ds(at, 16)
            moment_one, moment_two = new_moments(
                ahead_r[i, 0, rows].astype(F32),
                ahead_r[i, 1, rows].astype(F32),
                rot_s[i, rows].astype(F32),
            )
            dir_r[i, rows] = direction_of(moment_one, moment_two, one, two)

    loop(NF, direct_ahead)

    def direct(j, r):
        slot = slot_s[j]
        rows = pl.ds(KEEP + r * SLICE, SLICE)
        moment_one, moment_two = new_moments(
            mom_m[slot, rows], mom_v[slot, rows], rot_r[j, rows].astype(F32)
        )
        dir_s[j, pl.ds(r * SLICE, SLICE)] = direction_of(
            moment_one, moment_two, scale_one[slot], scale_two[slot]
        )

    def answer(n, r):
        j = from_nth(n)
        rows = pl.ds(KEEP + r * SLICE, SLICE)
        wait_bytes(rot_r.at[j, rows], rot_rs.at[r, j])
        direct(j, r)
        pltpu.make_async_remote_copy(
            src_ref=dir_s.at[j, pl.ds(r * SLICE, SLICE)],
            dst_ref=dir_r.at[me, rows],
            send_sem=dir_ss,
            recv_sem=dir_rs.at[me],
            device_id=peer(j),
            device_id_type=MESH,
        ).start()

    for r in range(BACK // SLICE):
        loop(NF - 1, lambda n, r=r: answer(n, r))
    loop(NF - 1, send_kept)
    for r in range(BACK // SLICE):
        direct(me, r)
    dir_r[me, pl.ds(KEEP, BACK)] = dir_s[me]

    def back_right(n):
        yy, rows = turn_rows(n)

        def arrive(xx):
            i = yy * SIDE + xx

            @pl.when(i != me)
            def _():
                wait_bytes(dir_r.at[i, pl.ds(KEEP, BACK)], dir_rs.at[i])

        loop(SIDE, arrive)
        half[rows, :] = lax.dot_general(
            dir_r[pl.ds(yy * SIDE, SIDE)].reshape(GROUP, BS),
            rmat[...],
            (((1,), (1,)), ((), ())),
            preferred_element_type=F32,
        ).astype(BF16)

    loop(SIDE - 1, back_right)

    def begin_left(q):
        rows = pl.ds(pl.multiple_of(q * GROUP, GROUP), GROUP)
        total = None
        for n in range(SIDE - 1):
            _, used = turn_rows(n)
            part_n = jnp.dot(lmat[rows, used], half[used, :], preferred_element_type=F32)
            total = part_n if total is None else total + part_n
        begun[rows, :] = total

    loop(SIDE, begin_left)
    back_right(SIDE - 1)

    def send_update(j, at):
        pltpu.make_async_remote_copy(
            src_ref=upd_s.at[j, pl.ds(at, PIECE)],
            dst_ref=upd_r.at[me, pl.ds(at, PIECE)],
            send_sem=upd_ss,
            recv_sem=upd_rs,
            device_id=peer(j),
            device_id_type=MESH,
        ).start()

    def back_left(n):
        yy, rows = turn_rows(n)
        _, last = turn_rows(SIDE - 1)
        upd_s[pl.ds(yy * SIDE, SIDE)] = (
            (begun[rows, :] + jnp.dot(lmat[rows, last], half[last, :], preferred_element_type=F32))
            .astype(BF16)
            .reshape(SIDE, ROWS, BS)
        )
        send_part(n, lambda j: send_update(j, 0))

    loop(SIDE, back_left)
    loop(NF - 1, lambda n: send_update(to_nth(n), PIECE))
    upd_r[me] = upd_s[me]

    wait_bytes(rot_r.at[pl.ds(0, NF - 1), pl.ds(0, KEEP)], kept_rs)

    def keep(b):
        owner = owner_s[b]
        for at in range(0, ROWS, SLICE):
            rows = pl.ds(at, SLICE)
            out_m[b, rows], out_v[b, rows] = new_moments(
                mom_m[b, rows], mom_v[b, rows], rot_r[owner, rows].astype(F32)
            )

    loop(NBD, keep)
    wait_bytes(upd_r.at[pl.ds(0, NF - 1)], upd_rs)

    def take(b):
        out_u[b] = upd_r[owner_s[b]]

    loop(NBD, take)

    wait_bytes(other, core_ss)
    wait_bytes(relay_s, relay_ss)
    wait_bytes(toward_s, toward_ss)
    wait_bytes(grad_s.at[:, pl.ds(0, NF - 1)], grad_ss)
    wait_bytes(ahead_s.at[pl.ds(0, NF - 1)], ahead_ss)
    wait_bytes(rot_s.at[pl.ds(0, NF - 1), pl.ds(KEEP, BACK)], rot_ss)
    wait_bytes(rot_s.at[pl.ds(0, NF - 1), pl.ds(0, KEEP)], kept_ss)
    wait_bytes(dir_s.at[pl.ds(0, NF - 1)], dir_ss)
    wait_bytes(upd_s.at[pl.ds(0, NF - 1)], upd_ss)


def shards(partials, first_moment, second_moment, step_counts, owners, left_basis, right_basis):
    part = partials.reshape(NZ, 2, NBD, ROWS, BS)
    strips = (NBD, ROWS, BS)
    slots = (NF, ROWS, BS)
    any_space = pl.BlockSpec(memory_space=pl.ANY)
    scalars = pl.BlockSpec(memory_space=pltpu.SMEM)
    dma = pltpu.SemaphoreType.DMA
    return pl.pallas_call(
        kernel,
        out_shape=(pltpu.VMEM(strips, BF16), pltpu.VMEM(strips, F32), pltpu.VMEM(strips, F32)),
        in_specs=[scalars] * 2 + [any_space] * 5,
        out_specs=(pl.BlockSpec(memory_space=pltpu.VMEM),) * 3,
        scratch_shapes=[
            pltpu.SMEM((NF,), jnp.int32),
            pltpu.SMEM((NBD,), jnp.int32),
            pltpu.VMEM((NBD, 1, BS), F32),
            pltpu.VMEM((NBD, 1, BS), F32),
            pltpu.VMEM((NCH, NZ, NBD, ROWS, CW), BF16),
            pltpu.VMEM((NCH, NZ, NBD, ROWS, CW), BF16),
            pltpu.VMEM((NCH, 2, NBD // 2, ROWS, CW), BF16),
            pltpu.VMEM((NCH, 2, NBD // 2, ROWS, CW), BF16),
            pltpu.VMEM((NCH, 2, NBD, ROWS, CW), BF16),
            pltpu.VMEM((NCH, 2, NBD, ROWS, CW), BF16),
            pltpu.VMEM((NBD, ROWS, CW), BF16),
            pltpu.VMEM((NCH, NF, ROWS, CW), BF16),
            pltpu.VMEM((NCH, NF, ROWS, CW), BF16),
            pltpu.VMEM((BS, BS), BF16),
            pltpu.VMEM((BS, BS), BF16),
            pltpu.VMEM((BS, BS), BF16),
            pltpu.VMEM((BS, BS), BF16),
            pltpu.VMEM((BS, BS), F32),
            pltpu.VMEM(strips, F32),
            pltpu.VMEM(strips, F32),
            pltpu.VMEM((NF, 2, KEEP, BS), BF16),
            pltpu.VMEM((NF, 2, KEEP, BS), BF16),
            pltpu.VMEM(slots, BF16),
            pltpu.VMEM(slots, BF16),
            pltpu.VMEM((NF, BACK, BS), BF16),
            pltpu.VMEM(slots, BF16),
            pltpu.VMEM(slots, BF16),
            pltpu.VMEM(slots, BF16),
            dma((NCH,)),
            dma((4,)),
            dma,
            dma((NCH, NZ)),
            dma,
            dma((NCH, 2)),
            dma,
            dma((NCH,)),
            dma,
            dma((NCH,)),
            dma,
            dma,
            dma,
            dma((BACK // SLICE, NF)),
            dma,
            dma,
            dma,
            dma((NF,)),
            dma,
            dma,
        ],
        compiler_params=pltpu.CompilerParams(
            collective_id=0, has_side_effects=True, vmem_limit_bytes=52 * 2**20
        ),
        name="soap_step",
    )(owners, step_counts, part, first_moment, second_moment, left_basis[0, 0], right_basis[0, 0])


def solution(mesh):
    placed = (
        P("dp", None, "fsdp", None),
        P("dp", "fsdp", None),
        P("dp", "fsdp", None),
        P(),
        P(),
        P("dp", "fsdp", None, None),
        P("dp", "fsdp", None, None),
    )
    return jax.shard_map(
        shards,
        mesh=mesh,
        in_specs=placed,
        out_specs=(P("dp", "fsdp", None), P("dp", "fsdp", None), P("dp", "fsdp", None)),
        check_vma=False,
    )
```

```python
import functools
import math

import jax
import jax.numpy as jnp
from jax import lax
from jax.experimental import pallas as pl
from jax.experimental.pallas import tpu as pltpu
from jax.sharding import PartitionSpec as P

BETA_ONE = 0.9
BETA_TWO = 0.95
EPSILON = 1e-08
MESH = pl.DeviceIdType.MESH
F32 = jnp.float32
BF16 = jnp.bfloat16

NZ = 4
SIDE = 4
NF = SIDE * SIDE
NBD = 8
ROWS = 64
BS = 1024
GROUP = SIDE * ROWS
NCH = 8
CW = BS // NCH
RELAY_LAG = 2
GRAD_LAG = 4
PAIR = 2
FIRST = BS - PAIR * CW
KEEP = 16
BACK = ROWS - KEEP
SLICE = 16
PIECE = ROWS // 4
TURNS = (2, 1, 3, 0)
PARTS = (
    ((2, 2), (2, 1), (2, 3)),
    ((1, 2), (1, 1), (1, 3)),
    ((3, 2), (3, 3), (3, 1), (2, 0)),
    ((0, 2), (1, 0), (3, 0), (0, 1), (0, 3)),
)
ORDER = sum(PARTS, ())


def new_moments(first, second, rotated):
    moment_one = BETA_ONE * first + (1.0 - BETA_ONE) * rotated
    moment_two = BETA_TWO * second + (1.0 - BETA_TWO) * (rotated * rotated)
    return moment_one, moment_two


def direction_of(moment_one, moment_two, scale_one, scale_two):
    return ((moment_one * scale_one) / (jnp.sqrt(moment_two * scale_two) + EPSILON)).astype(BF16)


def wait_bytes(ref, sem):
    pltpu.make_async_copy(ref, ref, sem).wait()


def kernel(
    owners, counts, part, first, second, left, right,
    out_u, out_m, out_v,
    slot_s, owner_s, scale_one, scale_two,
    own, other, relay_s, relay_r, toward_s, toward_r, summed, grad_s, grad_r,
    lmat, lturn, rmat, half, begun, mom_m, mom_v, ahead_s, ahead_r,
    rot_s, rot_r, dir_s, dir_r, upd_s, upd_r,
    ld_sem, in_sem, core_ss, core_rs, relay_ss, relay_rs, toward_ss, toward_rs,
    grad_ss, grad_rs, ahead_ss, ahead_rs, rot_ss, rot_rs, kept_ss, kept_rs, dir_ss, dir_rs, upd_ss, upd_rs,
):
    dp = lax.axis_index("dp")
    me = lax.axis_index("fsdp")
    z, core = dp // 2, dp % 2
    y, x = me // SIDE, me % SIDE
    up, down, far = (z + 1) % NZ, (z + NZ - 1) % NZ, (z + 2) % NZ
    dev_core = (z * 2 + 1 - core, me)
    dev_up = (up * 2 + core, me)
    dev_down = (down * 2 + core, me)

    def peer(index):
        return (dp, index)

    def loop(count, body):
        def step(i, carry):
            body(i)
            return carry

        lax.fori_loop(0, count, step, 0)

    def chosen(n, values):
        value = jnp.int32(values[0])
        for i, other_value in enumerate(values[1:]):
            value = jnp.where(n == i + 1, jnp.int32(other_value), value)
        return value

    def to_nth(n):
        yy = (y + chosen(n, [dy for dy, _ in ORDER])) % SIDE
        return yy * SIDE + (x + chosen(n, [dx for _, dx in ORDER])) % SIDE

    def from_nth(n):
        yy = (y + SIDE - chosen(n, [dy for dy, _ in ORDER])) % SIDE
        return yy * SIDE + (x + SIDE - chosen(n, [dx for _, dx in ORDER])) % SIDE

    def send_part(n, send):
        for i, part_n in enumerate(PARTS):

            @pl.when(n == i)
            def _():
                for dy, dx in part_n:
                    send(((y + dy) % SIDE) * SIDE + (x + dx) % SIDE)

    def turn_rows(n):
        yy = (y + chosen(n, TURNS)) % SIDE
        return yy, pl.ds(pl.multiple_of(yy * GROUP, GROUP), GROUP)

    def cols(k):
        return pl.ds(pl.multiple_of(k * CW, CW), CW)

    def load_own(k):
        return pltpu.make_async_copy(part.at[:, core, :, :, cols(k)], own.at[k], ld_sem.at[k])

    in_copies = [
        pltpu.make_async_copy(first, mom_m, in_sem.at[0]),
        pltpu.make_async_copy(second, mom_v, in_sem.at[1]),
        pltpu.make_async_copy(left, lmat, in_sem.at[2]),
        pltpu.make_async_copy(right, rmat, in_sem.at[3]),
    ]
    load_own(0).start()
    load_own(1).start()

    barrier = pltpu.get_barrier_semaphore()
    for device in (dev_core, dev_up, dev_down):
        pl.semaphore_signal(barrier, inc=1, device_id=device, device_id_type=MESH)

    def greet(d):
        pl.semaphore_signal(
            barrier, inc=1, device_id=peer((me + d + 1) % NF), device_id_type=MESH
        )

    loop(NF - 1, greet)

    def find_slots(j):
        slot = jnp.int32(0)
        for b in range(NBD):
            slot = jnp.where(owners[dp * NBD + b] == j, jnp.int32(b), slot)
        slot_s[j] = slot

    loop(NF, find_slots)

    def find_scales(b):
        owner_s[b] = owners[dp * NBD + b]
        count = jnp.full((1, BS), counts[dp * NBD + b].astype(F32), F32)
        scale_one[b] = 1.0 / (1.0 - jnp.exp(count * math.log(BETA_ONE)))
        scale_two[b] = 1.0 / (1.0 - jnp.exp(count * math.log(BETA_TWO)))

    loop(NBD, find_scales)
    pl.semaphore_wait(barrier, NF + 2)

    def send_core(k):
        for zz in (far, up, down, z):
            pltpu.make_async_remote_copy(
                src_ref=part.at[zz, 1 - core, :, :, cols(k)],
                dst_ref=other.at[k, zz],
                send_sem=core_ss,
                recv_sem=core_rs.at[k, zz],
                device_id=dev_core,
                device_id_type=MESH,
            ).start()

    def pair(k, zz, b):
        return own[k, zz, b].astype(F32) + other[k, zz, b].astype(F32)

    def send_toward(k, side, at, device):
        pltpu.make_async_remote_copy(
            src_ref=toward_s.at[k, side, pl.ds(at, NBD // 2)],
            dst_ref=toward_r.at[k, side, pl.ds(at, NBD // 2)],
            send_sem=toward_ss,
            recv_sem=toward_rs.at[k],
            device_id=device,
            device_id_type=MESH,
        ).start()

    hb = NBD // 2

    def sum_far(k):
        load_own(k).wait()
        wait_bytes(other.at[k, far], core_rs.at[k, far])
        for side, device in ((0, dev_up), (1, dev_down)):

            def body(b):
                relay_s[k, side, b] = pair(k, far, side * hb + b).astype(BF16)

            loop(hb, body)
            pltpu.make_async_remote_copy(
                src_ref=relay_s.at[k, side],
                dst_ref=relay_r.at[k, side],
                send_sem=relay_ss,
                recv_sem=relay_rs.at[k, side],
                device_id=device,
                device_id_type=MESH,
            ).start()

    def sum_near(k):
        for side, zz, device in ((0, up, dev_up), (1, down, dev_down)):
            wait_bytes(other.at[k, zz], core_rs.at[k, zz])
            at = (1 - side) * hb

            def body(b):
                toward_s[k, side, at + b] = pair(k, zz, at + b).astype(BF16)

            loop(hb, body)
            send_toward(k, side, at, device)

    def sum_relayed(k):
        for side, zz, device in ((0, up, dev_up), (1, down, dev_down)):
            wait_bytes(relay_r.at[k, side], relay_rs.at[k, side])
            at = side * hb

            def body(b):
                toward_s[k, side, at + b] = (
                    pair(k, zz, at + b) + relay_r[k, side, b].astype(F32)
                ).astype(BF16)

            loop(hb, body)
            send_toward(k, side, at, device)

    def send_grad(k):
        wait_bytes(other.at[k, z], core_rs.at[k, z])
        wait_bytes(toward_r.at[k], toward_rs.at[k])

        def body(b):
            summed[b] = (
                pair(k, z, b) + toward_r[k, 0, b].astype(F32) + toward_r[k, 1, b].astype(F32)
            ).astype(BF16)

        loop(NBD, body)

        def send(n):
            j = to_nth(n)
            grad_s[k, j] = summed[slot_s[j]]
            pltpu.make_async_remote_copy(
                src_ref=grad_s.at[k, j],
                dst_ref=grad_r.at[k, me],
                send_sem=grad_ss,
                recv_sem=grad_rs.at[k],
                device_id=peer(j),
                device_id_type=MESH,
            ).start()

        loop(NF - 1, send)
        grad_r[k, me] = summed[slot_s[me]]

    def turn_left(p):
        k = PAIR * p
        for n in range(PAIR):
            wait_bytes(grad_r.at[k + n, pl.ds(0, NF - 1)], grad_rs.at[k + n])

        def body(q):
            rows = pl.ds(pl.multiple_of(q * GROUP, GROUP), GROUP)
            grad = jnp.concatenate([grad_r[k + n].reshape(BS, CW) for n in range(PAIR)], axis=1)
            half[rows, pl.ds(pl.multiple_of(k * CW, PAIR * CW), PAIR * CW)] = jnp.dot(
                lturn[rows, :], grad, preferred_element_type=F32
            ).astype(BF16)

        loop(SIDE, body)

    def send_ahead():
        in_copies[0].wait()
        in_copies[1].wait()

        def pack(j):
            slot = slot_s[j]
            ahead_s[j, 0] = mom_m[slot][:KEEP].astype(BF16)
            ahead_s[j, 1] = mom_v[slot][:KEEP].astype(BF16)

        def send(n):
            j = to_nth(n)
            pack(j)
            pltpu.make_async_remote_copy(
                src_ref=ahead_s.at[j],
                dst_ref=ahead_r.at[me],
                send_sem=ahead_ss,
                recv_sem=ahead_rs,
                device_id=peer(j),
                device_id_type=MESH,
            ).start()

        loop(NF - 1, send)
        pack(me)
        ahead_r[me] = ahead_s[me]

    def turn_basis():
        in_copies[2].wait()
        in_copies[3].wait()

        def body(q):
            rows = pl.ds(pl.multiple_of(q * GROUP, GROUP), GROUP)
            lturn[rows, :] = lmat[:, rows].T

        loop(SIDE, body)

    def chunk(t):
        @pl.when(t + 2 < NCH)
        def _():
            load_own(t + 2).start()
            send_core(t + 2)

        @pl.when(t < NCH)
        def _():
            sum_far(t)
            sum_near(t)

        @pl.when(t == 0)
        def _():
            send_ahead()
            turn_basis()

        @pl.when((t >= RELAY_LAG) & (t < NCH + RELAY_LAG))
        def _():
            sum_relayed(t - RELAY_LAG)

        @pl.when(t >= GRAD_LAG)
        def _():
            send_grad(t - GRAD_LAG)

    send_core(0)
    send_core(1)
    for copy in in_copies:
        copy.start()
    loop(NCH + GRAD_LAG, chunk)
    loop(NCH // PAIR - 1, turn_left)

    def begin(q):
        rows = pl.ds(pl.multiple_of(q * GROUP, GROUP), GROUP)
        begun[rows, :] = jnp.dot(half[rows, :FIRST], rmat[:FIRST, :], preferred_element_type=F32)

    loop(SIDE, begin)
    turn_left(NCH // PAIR - 1)

    my_slot = slot_s[me]
    wait_bytes(ahead_r.at[pl.ds(0, NF - 1)], ahead_rs)

    def send_rotated(j, r):
        rows = pl.ds(KEEP + r * SLICE, SLICE)
        pltpu.make_async_remote_copy(
            src_ref=rot_s.at[j, rows],
            dst_ref=rot_r.at[me, rows],
            send_sem=rot_ss,
            recv_sem=rot_rs.at[r, me],
            device_id=peer(j),
            device_id_type=MESH,
        ).start()

    def send_kept(n):
        j = to_nth(n)
        pltpu.make_async_remote_copy(
            src_ref=rot_s.at[j, pl.ds(0, KEEP)],
            dst_ref=rot_r.at[me, pl.ds(0, KEEP)],
            send_sem=kept_ss,
            recv_sem=kept_rs,
            device_id=peer(j),
            device_id_type=MESH,
        ).start()

    def turn_right(n):
        yy, rows = turn_rows(n)
        rot_s[pl.ds(yy * SIDE, SIDE)] = (
            (begun[rows, :] + jnp.dot(half[rows, FIRST:], rmat[FIRST:, :], preferred_element_type=F32))
            .astype(BF16)
            .reshape(SIDE, ROWS, BS)
        )
        send_part(n, lambda j: send_rotated(j, 0))

    loop(SIDE, turn_right)
    for r in range(1, BACK // SLICE):
        loop(NF - 1, lambda n, r=r: send_rotated(to_nth(n), r))
    rot_r[me] = rot_s[me]

    def direct_ahead(i):
        one, two = scale_one[my_slot], scale_two[my_slot]
        for at in range(0, KEEP, 16):
            rows = pl.ds(at, 16)
            moment_one, moment_two = new_moments(
                ahead_r[i, 0, rows].astype(F32),
                ahead_r[i, 1, rows].astype(F32),
                rot_s[i, rows].astype(F32),
            )
            dir_r[i, rows] = direction_of(moment_one, moment_two, one, two)

    loop(NF, direct_ahead)

    def direct(j, r):
        slot = slot_s[j]
        rows = pl.ds(KEEP + r * SLICE, SLICE)
        moment_one, moment_two = new_moments(
            mom_m[slot, rows], mom_v[slot, rows], rot_r[j, rows].astype(F32)
        )
        dir_s[j, pl.ds(r * SLICE, SLICE)] = direction_of(
            moment_one, moment_two, scale_one[slot], scale_two[slot]
        )

    def answer(n, r):
        j = from_nth(n)
        rows = pl.ds(KEEP + r * SLICE, SLICE)
        wait_bytes(rot_r.at[j, rows], rot_rs.at[r, j])
        direct(j, r)
        pltpu.make_async_remote_copy(
            src_ref=dir_s.at[j, pl.ds(r * SLICE, SLICE)],
            dst_ref=dir_r.at[me, rows],
            send_sem=dir_ss,
            recv_sem=dir_rs.at[me],
            device_id=peer(j),
            device_id_type=MESH,
        ).start()

    for r in range(BACK // SLICE):
        loop(NF - 1, lambda n, r=r: answer(n, r))
    loop(NF - 1, send_kept)
    for r in range(BACK // SLICE):
        direct(me, r)
    dir_r[me, pl.ds(KEEP, BACK)] = dir_s[me]

    def back_right(n):
        yy, rows = turn_rows(n)

        def arrive(xx):
            i = yy * SIDE + xx

            @pl.when(i != me)
            def _():
                wait_bytes(dir_r.at[i, pl.ds(KEEP, BACK)], dir_rs.at[i])

        loop(SIDE, arrive)
        half[rows, :] = lax.dot_general(
            dir_r[pl.ds(yy * SIDE, SIDE)].reshape(GROUP, BS),
            rmat[...],
            (((1,), (1,)), ((), ())),
            preferred_element_type=F32,
        ).astype(BF16)

    loop(SIDE - 1, back_right)

    def begin_left(q):
        rows = pl.ds(pl.multiple_of(q * GROUP, GROUP), GROUP)
        total = None
        for n in range(SIDE - 1):
            _, used = turn_rows(n)
            part_n = jnp.dot(lmat[rows, used], half[used, :], preferred_element_type=F32)
            total = part_n if total is None else total + part_n
        begun[rows, :] = total

    loop(SIDE, begin_left)
    back_right(SIDE - 1)

    def send_update(j, at):
        pltpu.make_async_remote_copy(
            src_ref=upd_s.at[j, pl.ds(at, PIECE)],
            dst_ref=upd_r.at[me, pl.ds(at, PIECE)],
            send_sem=upd_ss,
            recv_sem=upd_rs,
            device_id=peer(j),
            device_id_type=MESH,
        ).start()

    def back_left(n):
        yy, rows = turn_rows(n)
        _, last = turn_rows(SIDE - 1)
        upd_s[pl.ds(yy * SIDE, SIDE)] = (
            (begun[rows, :] + jnp.dot(lmat[rows, last], half[last, :], preferred_element_type=F32))
            .astype(BF16)
            .reshape(SIDE, ROWS, BS)
        )
        send_part(n, lambda j: send_update(j, 0))

    loop(SIDE, back_left)
    for at in range(PIECE, ROWS, PIECE):
        loop(NF - 1, lambda n, at=at: send_update(to_nth(n), at))
    upd_r[me] = upd_s[me]

    wait_bytes(rot_r.at[pl.ds(0, NF - 1), pl.ds(0, KEEP)], kept_rs)

    def keep(b):
        owner = owner_s[b]
        for at in range(0, ROWS, SLICE):
            rows = pl.ds(at, SLICE)
            out_m[b, rows], out_v[b, rows] = new_moments(
                mom_m[b, rows], mom_v[b, rows], rot_r[owner, rows].astype(F32)
            )

    loop(NBD, keep)
    wait_bytes(upd_r.at[pl.ds(0, NF - 1)], upd_rs)

    def take(b):
        out_u[b] = upd_r[owner_s[b]]

    loop(NBD, take)

    wait_bytes(other, core_ss)
    wait_bytes(relay_s, relay_ss)
    wait_bytes(toward_s, toward_ss)
    wait_bytes(grad_s.at[:, pl.ds(0, NF - 1)], grad_ss)
    wait_bytes(ahead_s.at[pl.ds(0, NF - 1)], ahead_ss)
    wait_bytes(rot_s.at[pl.ds(0, NF - 1), pl.ds(KEEP, BACK)], rot_ss)
    wait_bytes(rot_s.at[pl.ds(0, NF - 1), pl.ds(0, KEEP)], kept_ss)
    wait_bytes(dir_s.at[pl.ds(0, NF - 1)], dir_ss)
    wait_bytes(upd_s.at[pl.ds(0, NF - 1)], upd_ss)


def shards(partials, first_moment, second_moment, step_counts, owners, left_basis, right_basis):
    part = partials.reshape(NZ, 2, NBD, ROWS, BS)
    strips = (NBD, ROWS, BS)
    slots = (NF, ROWS, BS)
    any_space = pl.BlockSpec(memory_space=pl.ANY)
    scalars = pl.BlockSpec(memory_space=pltpu.SMEM)
    dma = pltpu.SemaphoreType.DMA
    return pl.pallas_call(
        kernel,
        out_shape=(pltpu.VMEM(strips, BF16), pltpu.VMEM(strips, F32), pltpu.VMEM(strips, F32)),
        in_specs=[scalars] * 2 + [any_space] * 5,
        out_specs=(pl.BlockSpec(memory_space=pltpu.VMEM),) * 3,
        scratch_shapes=[
            pltpu.SMEM((NF,), jnp.int32),
            pltpu.SMEM((NBD,), jnp.int32),
            pltpu.VMEM((NBD, 1, BS), F32),
            pltpu.VMEM((NBD, 1, BS), F32),
            pltpu.VMEM((NCH, NZ, NBD, ROWS, CW), BF16),
            pltpu.VMEM((NCH, NZ, NBD, ROWS, CW), BF16),
            pltpu.VMEM((NCH, 2, NBD // 2, ROWS, CW), BF16),
            pltpu.VMEM((NCH, 2, NBD // 2, ROWS, CW), BF16),
            pltpu.VMEM((NCH, 2, NBD, ROWS, CW), BF16),
            pltpu.VMEM((NCH, 2, NBD, ROWS, CW), BF16),
            pltpu.VMEM((NBD, ROWS, CW), BF16),
            pltpu.VMEM((NCH, NF, ROWS, CW), BF16),
            pltpu.VMEM((NCH, NF, ROWS, CW), BF16),
            pltpu.VMEM((BS, BS), BF16),
            pltpu.VMEM((BS, BS), BF16),
            pltpu.VMEM((BS, BS), BF16),
            pltpu.VMEM((BS, BS), BF16),
            pltpu.VMEM((BS, BS), F32),
            pltpu.VMEM(strips, F32),
            pltpu.VMEM(strips, F32),
            pltpu.VMEM((NF, 2, KEEP, BS), BF16),
            pltpu.VMEM((NF, 2, KEEP, BS), BF16),
            pltpu.VMEM(slots, BF16),
            pltpu.VMEM(slots, BF16),
            pltpu.VMEM((NF, BACK, BS), BF16),
            pltpu.VMEM(slots, BF16),
            pltpu.VMEM(slots, BF16),
            pltpu.VMEM(slots, BF16),
            dma((NCH,)),
            dma((4,)),
            dma,
            dma((NCH, NZ)),
            dma,
            dma((NCH, 2)),
            dma,
            dma((NCH,)),
            dma,
            dma((NCH,)),
            dma,
            dma,
            dma,
            dma((BACK // SLICE, NF)),
            dma,
            dma,
            dma,
            dma((NF,)),
            dma,
            dma,
        ],
        compiler_params=pltpu.CompilerParams(
            collective_id=0, has_side_effects=True, vmem_limit_bytes=52 * 2**20
        ),
        name="soap_step",
    )(owners, step_counts, part, first_moment, second_moment, left_basis[0, 0], right_basis[0, 0])


def solution(mesh):
    placed = (
        P("dp", None, "fsdp", None),
        P("dp", "fsdp", None),
        P("dp", "fsdp", None),
        P(),
        P(),
        P("dp", "fsdp", None, None),
        P("dp", "fsdp", None, None),
    )
    return jax.shard_map(
        shards,
        mesh=mesh,
        in_specs=placed,
        out_specs=(P("dp", "fsdp", None), P("dp", "fsdp", None), P("dp", "fsdp", None)),
        check_vma=False,
    )
```

```python
import functools
import math

import jax
import jax.numpy as jnp
from jax import lax
from jax.experimental import pallas as pl
from jax.experimental.pallas import tpu as pltpu
from jax.sharding import PartitionSpec as P

BETA_ONE = 0.9
BETA_TWO = 0.95
EPSILON = 1e-08
MESH = pl.DeviceIdType.MESH
F32 = jnp.float32
BF16 = jnp.bfloat16

NZ = 4
SIDE = 4
NF = SIDE * SIDE
NBD = 8
ROWS = 64
BS = 1024
GROUP = SIDE * ROWS
NCH = 8
CW = BS // NCH
RELAY_LAG = 2
GRAD_LAG = 4
PAIR = 2
FIRST = BS - PAIR * CW
KEEP = 16
BACK = ROWS - KEEP
SLICE = 16
PIECE = ROWS // 4
TURNS = (2, 1, 3, 0)
PARTS = (
    ((2, 2), (2, 1), (2, 3)),
    ((1, 2), (1, 1), (1, 3)),
    ((3, 2), (3, 3), (3, 1), (2, 0)),
    ((0, 2), (1, 0), (3, 0), (0, 1), (0, 3)),
)
ORDER = sum(PARTS, ())


def new_moments(first, second, rotated):
    moment_one = BETA_ONE * first + (1.0 - BETA_ONE) * rotated
    moment_two = BETA_TWO * second + (1.0 - BETA_TWO) * (rotated * rotated)
    return moment_one, moment_two


def direction_of(moment_one, moment_two, scale_one, scale_two):
    return ((moment_one * scale_one) / (jnp.sqrt(moment_two * scale_two) + EPSILON)).astype(BF16)


def wait_bytes(ref, sem):
    pltpu.make_async_copy(ref, ref, sem).wait()


def kernel(
    owners, counts, part, first, second, left, right,
    out_u, out_m, out_v,
    slot_s, owner_s, scale_one, scale_two,
    own, other, relay_s, relay_r, toward_s, toward_r, summed, grad_s, grad_r,
    lmat, lturn, rmat, half, begun, mom_m, mom_v, ahead_s, ahead_r,
    rot_s, rot_r, dir_s, dir_r, upd_s, upd_r,
    ld_sem, in_sem, core_ss, core_rs, relay_ss, relay_rs, toward_ss, toward_rs,
    grad_ss, grad_rs, ahead_ss, ahead_rs, rot_ss, rot_rs, kept_ss, kept_rs, dir_ss, dir_rs, upd_ss, upd_rs,
):
    dp = lax.axis_index("dp")
    me = lax.axis_index("fsdp")
    z, core = dp // 2, dp % 2
    y, x = me // SIDE, me % SIDE
    up, down, far = (z + 1) % NZ, (z + NZ - 1) % NZ, (z + 2) % NZ
    dev_core = (z * 2 + 1 - core, me)
    dev_up = (up * 2 + core, me)
    dev_down = (down * 2 + core, me)

    def peer(index):
        return (dp, index)

    def loop(count, body):
        def step(i, carry):
            body(i)
            return carry

        lax.fori_loop(0, count, step, 0)

    def chosen(n, values):
        value = jnp.int32(values[0])
        for i, other_value in enumerate(values[1:]):
            value = jnp.where(n == i + 1, jnp.int32(other_value), value)
        return value

    def to_nth(n):
        yy = (y + chosen(n, [dy for dy, _ in ORDER])) % SIDE
        return yy * SIDE + (x + chosen(n, [dx for _, dx in ORDER])) % SIDE

    def from_nth(n):
        yy = (y + SIDE - chosen(n, [dy for dy, _ in ORDER])) % SIDE
        return yy * SIDE + (x + SIDE - chosen(n, [dx for _, dx in ORDER])) % SIDE

    def send_part(n, send):
        for i, part_n in enumerate(PARTS):

            @pl.when(n == i)
            def _():
                for dy, dx in part_n:
                    send(((y + dy) % SIDE) * SIDE + (x + dx) % SIDE)

    def turn_rows(n):
        yy = (y + chosen(n, TURNS)) % SIDE
        return yy, pl.ds(pl.multiple_of(yy * GROUP, GROUP), GROUP)

    def cols(k):
        return pl.ds(pl.multiple_of(k * CW, CW), CW)

    def load_own(k):
        return pltpu.make_async_copy(part.at[:, core, :, :, cols(k)], own.at[k], ld_sem.at[k])

    in_copies = [
        pltpu.make_async_copy(first, mom_m, in_sem.at[0]),
        pltpu.make_async_copy(second, mom_v, in_sem.at[1]),
        pltpu.make_async_copy(left, lmat, in_sem.at[2]),
        pltpu.make_async_copy(right, rmat, in_sem.at[3]),
    ]
    load_own(0).start()
    load_own(1).start()

    barrier = pltpu.get_barrier_semaphore()
    for device in (dev_core, dev_up, dev_down):
        pl.semaphore_signal(barrier, inc=1, device_id=device, device_id_type=MESH)

    def greet(d):
        pl.semaphore_signal(
            barrier, inc=1, device_id=peer((me + d + 1) % NF), device_id_type=MESH
        )

    loop(NF - 1, greet)

    def find_slots(j):
        slot = jnp.int32(0)
        for b in range(NBD):
            slot = jnp.where(owners[dp * NBD + b] == j, jnp.int32(b), slot)
        slot_s[j] = slot

    loop(NF, find_slots)

    def find_scales(b):
        owner_s[b] = owners[dp * NBD + b]
        count = jnp.full((1, BS), counts[dp * NBD + b].astype(F32), F32)
        scale_one[b] = 1.0 / (1.0 - jnp.exp(count * math.log(BETA_ONE)))
        scale_two[b] = 1.0 / (1.0 - jnp.exp(count * math.log(BETA_TWO)))

    loop(NBD, find_scales)
    pl.semaphore_wait(barrier, NF + 2)

    def send_core(k):
        for zz in (far, up, down, z):
            pltpu.make_async_remote_copy(
                src_ref=part.at[zz, 1 - core, :, :, cols(k)],
                dst_ref=other.at[k, zz],
                send_sem=core_ss,
                recv_sem=core_rs.at[k, zz],
                device_id=dev_core,
                device_id_type=MESH,
            ).start()

    def pair(k, zz, b):
        return own[k, zz, b].astype(F32) + other[k, zz, b].astype(F32)

    def send_toward(k, side, at, device):
        pltpu.make_async_remote_copy(
            src_ref=toward_s.at[k, side, pl.ds(at, NBD // 2)],
            dst_ref=toward_r.at[k, side, pl.ds(at, NBD // 2)],
            send_sem=toward_ss,
            recv_sem=toward_rs.at[k],
            device_id=device,
            device_id_type=MESH,
        ).start()

    hb = NBD // 2

    def sum_far(k):
        load_own(k).wait()
        wait_bytes(other.at[k, far], core_rs.at[k, far])
        for side, device in ((0, dev_up), (1, dev_down)):

            def body(b):
                relay_s[k, side, b] = pair(k, far, side * hb + b).astype(BF16)

            loop(hb, body)
            pltpu.make_async_remote_copy(
                src_ref=relay_s.at[k, side],
                dst_ref=relay_r.at[k, side],
                send_sem=relay_ss,
                recv_sem=relay_rs.at[k, side],
                device_id=device,
                device_id_type=MESH,
            ).start()

    def sum_near(k):
        for side, zz, device in ((0, up, dev_up), (1, down, dev_down)):
            wait_bytes(other.at[k, zz], core_rs.at[k, zz])
            at = (1 - side) * hb

            def body(b):
                toward_s[k, side, at + b] = pair(k, zz, at + b).astype(BF16)

            loop(hb, body)
            send_toward(k, side, at, device)

    def sum_relayed(k):
        for side, zz, device in ((0, up, dev_up), (1, down, dev_down)):
            wait_bytes(relay_r.at[k, side], relay_rs.at[k, side])
            at = side * hb

            def body(b):
                toward_s[k, side, at + b] = (
                    pair(k, zz, at + b) + relay_r[k, side, b].astype(F32)
                ).astype(BF16)

            loop(hb, body)
            send_toward(k, side, at, device)

    def send_grad(k):
        wait_bytes(other.at[k, z], core_rs.at[k, z])
        wait_bytes(toward_r.at[k], toward_rs.at[k])

        def body(b):
            summed[b] = (
                pair(k, z, b) + toward_r[k, 0, b].astype(F32) + toward_r[k, 1, b].astype(F32)
            ).astype(BF16)

        loop(NBD, body)

        def send(n):
            j = to_nth(n)
            grad_s[k, j] = summed[slot_s[j]]
            pltpu.make_async_remote_copy(
                src_ref=grad_s.at[k, j],
                dst_ref=grad_r.at[k, me],
                send_sem=grad_ss,
                recv_sem=grad_rs.at[k],
                device_id=peer(j),
                device_id_type=MESH,
            ).start()

        loop(NF - 1, send)
        grad_r[k, me] = summed[slot_s[me]]

    def turn_left(p):
        k = PAIR * p
        for n in range(PAIR):
            wait_bytes(grad_r.at[k + n, pl.ds(0, NF - 1)], grad_rs.at[k + n])

        def body(q):
            rows = pl.ds(pl.multiple_of(q * GROUP, GROUP), GROUP)
            grad = jnp.concatenate([grad_r[k + n].reshape(BS, CW) for n in range(PAIR)], axis=1)
            half[rows, pl.ds(pl.multiple_of(k * CW, PAIR * CW), PAIR * CW)] = jnp.dot(
                lturn[rows, :], grad, preferred_element_type=F32
            ).astype(BF16)

        loop(SIDE, body)

    def send_ahead():
        in_copies[0].wait()
        in_copies[1].wait()

        def pack(j):
            slot = slot_s[j]
            ahead_s[j, 0] = mom_m[slot][:KEEP].astype(BF16)
            ahead_s[j, 1] = mom_v[slot][:KEEP].astype(BF16)

        def send(n):
            j = to_nth(n)
            pack(j)
            pltpu.make_async_remote_copy(
                src_ref=ahead_s.at[j],
                dst_ref=ahead_r.at[me],
                send_sem=ahead_ss,
                recv_sem=ahead_rs,
                device_id=peer(j),
                device_id_type=MESH,
            ).start()

        loop(NF - 1, send)
        pack(me)
        ahead_r[me] = ahead_s[me]

    def turn_basis():
        in_copies[2].wait()
        in_copies[3].wait()

        def body(q):
            rows = pl.ds(pl.multiple_of(q * GROUP, GROUP), GROUP)
            lturn[rows, :] = lmat[:, rows].T

        loop(SIDE, body)

    def chunk(t):
        @pl.when(t + 2 < NCH)
        def _():
            load_own(t + 2).start()
            send_core(t + 2)

        @pl.when(t < NCH)
        def _():
            sum_far(t)
            sum_near(t)

        @pl.when(t == 0)
        def _():
            send_ahead()
            turn_basis()

        @pl.when((t >= RELAY_LAG) & (t < NCH + RELAY_LAG))
        def _():
            sum_relayed(t - RELAY_LAG)

        @pl.when(t >= GRAD_LAG)
        def _():
            send_grad(t - GRAD_LAG)

    send_core(0)
    send_core(1)
    for copy in in_copies:
        copy.start()
    loop(NCH + GRAD_LAG, chunk)
    loop(NCH // PAIR - 1, turn_left)

    def begin(q):
        rows = pl.ds(pl.multiple_of(q * GROUP, GROUP), GROUP)
        begun[rows, :] = jnp.dot(half[rows, :FIRST], rmat[:FIRST, :], preferred_element_type=F32)

    loop(SIDE, begin)
    turn_left(NCH // PAIR - 1)

    my_slot = slot_s[me]
    wait_bytes(ahead_r.at[pl.ds(0, NF - 1)], ahead_rs)

    def send_rotated(j, r):
        rows = pl.ds(KEEP + r * SLICE, SLICE)
        pltpu.make_async_remote_copy(
            src_ref=rot_s.at[j, rows],
            dst_ref=rot_r.at[me, rows],
            send_sem=rot_ss,
            recv_sem=rot_rs.at[r, me],
            device_id=peer(j),
            device_id_type=MESH,
        ).start()

    def send_kept(n):
        j = to_nth(n)
        pltpu.make_async_remote_copy(
            src_ref=rot_s.at[j, pl.ds(0, KEEP)],
            dst_ref=rot_r.at[me, pl.ds(0, KEEP)],
            send_sem=kept_ss,
            recv_sem=kept_rs,
            device_id=peer(j),
            device_id_type=MESH,
        ).start()

    def turn_right(n):
        yy, rows = turn_rows(n)
        rot_s[pl.ds(yy * SIDE, SIDE)] = (
            (begun[rows, :] + jnp.dot(half[rows, FIRST:], rmat[FIRST:, :], preferred_element_type=F32))
            .astype(BF16)
            .reshape(SIDE, ROWS, BS)
        )
        send_part(n, lambda j: send_rotated(j, 0))

    loop(SIDE, turn_right)
    for r in range(1, BACK // SLICE):
        loop(NF - 1, lambda n, r=r: send_rotated(to_nth(n), r))
    rot_r[me] = rot_s[me]

    def direct_ahead(i):
        one, two = scale_one[my_slot], scale_two[my_slot]
        for at in range(0, KEEP, 16):
            rows = pl.ds(at, 16)
            moment_one, moment_two = new_moments(
                ahead_r[i, 0, rows].astype(F32),
                ahead_r[i, 1, rows].astype(F32),
                rot_s[i, rows].astype(F32),
            )
            dir_r[i, rows] = direction_of(moment_one, moment_two, one, two)

    loop(NF, direct_ahead)

    def direct(j, r):
        slot = slot_s[j]
        rows = pl.ds(KEEP + r * SLICE, SLICE)
        moment_one, moment_two = new_moments(
            mom_m[slot, rows], mom_v[slot, rows], rot_r[j, rows].astype(F32)
        )
        dir_s[j, pl.ds(r * SLICE, SLICE)] = direction_of(
            moment_one, moment_two, scale_one[slot], scale_two[slot]
        )

    def answer(n, r):
        j = from_nth(n)
        rows = pl.ds(KEEP + r * SLICE, SLICE)
        wait_bytes(rot_r.at[j, rows], rot_rs.at[r, j])
        direct(j, r)
        pltpu.make_async_remote_copy(
            src_ref=dir_s.at[j, pl.ds(r * SLICE, SLICE)],
            dst_ref=dir_r.at[me, rows],
            send_sem=dir_ss,
            recv_sem=dir_rs.at[me],
            device_id=peer(j),
            device_id_type=MESH,
        ).start()

    for r in range(BACK // SLICE):
        loop(NF - 1, lambda n, r=r: answer(n, r))
    loop(NF - 1, send_kept)
    for r in range(BACK // SLICE):
        direct(me, r)
    dir_r[me, pl.ds(KEEP, BACK)] = dir_s[me]

    def back_right(n):
        yy, rows = turn_rows(n)

        def arrive(xx):
            i = yy * SIDE + xx

            @pl.when(i != me)
            def _():
                wait_bytes(dir_r.at[i, pl.ds(KEEP, BACK)], dir_rs.at[i])

        loop(SIDE, arrive)
        half[rows, :] = lax.dot_general(
            dir_r[pl.ds(yy * SIDE, SIDE)].reshape(GROUP, BS),
            rmat[...],
            (((1,), (1,)), ((), ())),
            preferred_element_type=F32,
        ).astype(BF16)

    loop(SIDE // 2, back_right)

    def begin_left(q):
        rows = pl.ds(pl.multiple_of(q * GROUP, GROUP), GROUP)
        total = None
        for n in range(SIDE // 2):
            _, used = turn_rows(n)
            part_n = jnp.dot(lmat[rows, used], half[used, :], preferred_element_type=F32)
            total = part_n if total is None else total + part_n
        begun[rows, :] = total

    loop(SIDE, begin_left)
    loop(SIDE // 2, lambda n: back_right(n + SIDE // 2))

    def send_update(j, at):
        pltpu.make_async_remote_copy(
            src_ref=upd_s.at[j, pl.ds(at, PIECE)],
            dst_ref=upd_r.at[me, pl.ds(at, PIECE)],
            send_sem=upd_ss,
            recv_sem=upd_rs,
            device_id=peer(j),
            device_id_type=MESH,
        ).start()

    def back_left(n):
        yy, rows = turn_rows(n)
        total = begun[rows, :]
        for m in range(SIDE // 2, SIDE):
            _, used = turn_rows(m)
            total += jnp.dot(lmat[rows, used], half[used, :], preferred_element_type=F32)
        upd_s[pl.ds(yy * SIDE, SIDE)] = (
            total.astype(BF16)
            .reshape(SIDE, ROWS, BS)
        )
        send_part(n, lambda j: send_update(j, 0))

    loop(SIDE, back_left)
    for at in range(PIECE, ROWS, PIECE):
        loop(NF - 1, lambda n, at=at: send_update(to_nth(n), at))
    upd_r[me] = upd_s[me]

    wait_bytes(rot_r.at[pl.ds(0, NF - 1), pl.ds(0, KEEP)], kept_rs)

    def keep(b):
        owner = owner_s[b]
        for at in range(0, ROWS, SLICE):
            rows = pl.ds(at, SLICE)
            out_m[b, rows], out_v[b, rows] = new_moments(
                mom_m[b, rows], mom_v[b, rows], rot_r[owner, rows].astype(F32)
            )

    loop(NBD, keep)
    wait_bytes(upd_r.at[pl.ds(0, NF - 1)], upd_rs)

    def take(b):
        out_u[b] = upd_r[owner_s[b]]

    loop(NBD, take)

    wait_bytes(other, core_ss)
    wait_bytes(relay_s, relay_ss)
    wait_bytes(toward_s, toward_ss)
    wait_bytes(grad_s.at[:, pl.ds(0, NF - 1)], grad_ss)
    wait_bytes(ahead_s.at[pl.ds(0, NF - 1)], ahead_ss)
    wait_bytes(rot_s.at[pl.ds(0, NF - 1), pl.ds(KEEP, BACK)], rot_ss)
    wait_bytes(rot_s.at[pl.ds(0, NF - 1), pl.ds(0, KEEP)], kept_ss)
    wait_bytes(dir_s.at[pl.ds(0, NF - 1)], dir_ss)
    wait_bytes(upd_s.at[pl.ds(0, NF - 1)], upd_ss)


def shards(partials, first_moment, second_moment, step_counts, owners, left_basis, right_basis):
    part = partials.reshape(NZ, 2, NBD, ROWS, BS)
    strips = (NBD, ROWS, BS)
    slots = (NF, ROWS, BS)
    any_space = pl.BlockSpec(memory_space=pl.ANY)
    scalars = pl.BlockSpec(memory_space=pltpu.SMEM)
    dma = pltpu.SemaphoreType.DMA
    return pl.pallas_call(
        kernel,
        out_shape=(pltpu.VMEM(strips, BF16), pltpu.VMEM(strips, F32), pltpu.VMEM(strips, F32)),
        in_specs=[scalars] * 2 + [any_space] * 5,
        out_specs=(pl.BlockSpec(memory_space=pltpu.VMEM),) * 3,
        scratch_shapes=[
            pltpu.SMEM((NF,), jnp.int32),
            pltpu.SMEM((NBD,), jnp.int32),
            pltpu.VMEM((NBD, 1, BS), F32),
            pltpu.VMEM((NBD, 1, BS), F32),
            pltpu.VMEM((NCH, NZ, NBD, ROWS, CW), BF16),
            pltpu.VMEM((NCH, NZ, NBD, ROWS, CW), BF16),
            pltpu.VMEM((NCH, 2, NBD // 2, ROWS, CW), BF16),
            pltpu.VMEM((NCH, 2, NBD // 2, ROWS, CW), BF16),
            pltpu.VMEM((NCH, 2, NBD, ROWS, CW), BF16),
            pltpu.VMEM((NCH, 2, NBD, ROWS, CW), BF16),
            pltpu.VMEM((NBD, ROWS, CW), BF16),
            pltpu.VMEM((NCH, NF, ROWS, CW), BF16),
            pltpu.VMEM((NCH, NF, ROWS, CW), BF16),
            pltpu.VMEM((BS, BS), BF16),
            pltpu.VMEM((BS, BS), BF16),
            pltpu.VMEM((BS, BS), BF16),
            pltpu.VMEM((BS, BS), BF16),
            pltpu.VMEM((BS, BS), F32),
            pltpu.VMEM(strips, F32),
            pltpu.VMEM(strips, F32),
            pltpu.VMEM((NF, 2, KEEP, BS), BF16),
            pltpu.VMEM((NF, 2, KEEP, BS), BF16),
            pltpu.VMEM(slots, BF16),
            pltpu.VMEM(slots, BF16),
            pltpu.VMEM((NF, BACK, BS), BF16),
            pltpu.VMEM(slots, BF16),
            pltpu.VMEM(slots, BF16),
            pltpu.VMEM(slots, BF16),
            dma((NCH,)),
            dma((4,)),
            dma,
            dma((NCH, NZ)),
            dma,
            dma((NCH, 2)),
            dma,
            dma((NCH,)),
            dma,
            dma((NCH,)),
            dma,
            dma,
            dma,
            dma((BACK // SLICE, NF)),
            dma,
            dma,
            dma,
            dma((NF,)),
            dma,
            dma,
        ],
        compiler_params=pltpu.CompilerParams(
            collective_id=0, has_side_effects=True, vmem_limit_bytes=52 * 2**20
        ),
        name="soap_step",
    )(owners, step_counts, part, first_moment, second_moment, left_basis[0, 0], right_basis[0, 0])


def solution(mesh):
    placed = (
        P("dp", None, "fsdp", None),
        P("dp", "fsdp", None),
        P("dp", "fsdp", None),
        P(),
        P(),
        P("dp", "fsdp", None, None),
        P("dp", "fsdp", None, None),
    )
    return jax.shard_map(
        shards,
        mesh=mesh,
        in_specs=placed,
        out_specs=(P("dp", "fsdp", None), P("dp", "fsdp", None), P("dp", "fsdp", None)),
        check_vma=False,
    )
```
